256 devices in a mesh: group: 8 (over x, core), local: 32 (over z, y).
Axes of the slice: x: 4, y: 4, z: 8, core: 2. Of those that a mesh axis runs over, the one named last changes fastest.
Arguments:
- coords: float32 [3, 262144], P(None, ('group', 'local')), may hold values from -6 to 6
- inv_length: float32 [3], replicated, may hold values from 0.5 to 2
- noise: float32 [262144], P(('group', 'local')), may hold values from 1 to 4
- order: int32 [256, 1024], P(('group', 'local')), may hold values from 0 to 1023, each once within a row
- basis: bfloat16 [262144, 8, 256], P(('group', 'local')), may hold values from -6 to 6
- probes: float32 [128, 262144], P(None, ('group', 'local')), may hold values from -8 to 8
Outputs:
- solution: float32 [128, 262144], P(None, ('group', 'local'))
- residual: float32 [128, 262144], P(None, ('group', 'local'))
The draws below stay inside these ranges and needn't reach their ends.
All inputs are finite; a program needn't handle non-finite values.
Results may differ from the reference program's by a relative error of at most 0.0003.
Values sent between devices are 32-bit elements; how exact they have to be, the bound alone decides.
No kernel may reach another device: no remote copies, remote signals or barrier semaphores. Data moves between devices by JAX's collectives and lax.ppermute only.
A program may use at most 64 MiB of HBM per device.

```python
import math
import jax
import jax.numpy as jnp
from jax import lax

LEAF = 1024
RANK = 256
PROBES = 128
ITERS = 2
LEVELS = 8
POINTS = 262144
DEVICES = 256


def steps_of(own_key, extent, shards, least, high):
    def one(dim, shards_of):
        heights = jax.random.uniform(jax.random.fold_in(jax.random.fold_in(own_key, 6), dim), (shards_of,), jnp.float32, least / len(shards), high / len(shards))
        return jnp.repeat(jnp.exp(heights), extent[dim] // shards_of).reshape((-1,) + (1,) * (len(extent) - dim - 1))

    gain = one(*shards[0])
    for cut in shards[1:]:
        gain = gain * one(*cut)
    return gain


def centred(rng, extent, deviation, bound, cuts=(), kind=jnp.bfloat16):
    drawn = jax.random.normal(rng, extent, jnp.float32) * deviation
    if len(cuts) > 0:
        drawn = steps_of(rng, extent, cuts, -0.22, 0.18) * drawn
    return jnp.clip(drawn, min=-bound, max=bound).astype(kind)


def setup_inputs(seed: int = 0) -> dict:
    seeds = jax.random.split(jax.random.key(seed), 7)
    coords = centred(seeds[0], (3, POINTS), 1.0, 6.0, ((1, 256),), jnp.float32)
    inv_length = jnp.clip(jnp.exp(jax.random.uniform(seeds[1], (3,), jnp.float32, math.log(0.5), math.log(2.0))), 0.5, 2.0)
    noise = jnp.clip(jnp.exp(math.log(4.0) - 1.3862944 * jax.random.uniform(seeds[2], (POINTS,), jnp.float32) ** steps_of(seeds[2], (POINTS,), ((0, 256),), -0.2, 0.2)), 1.0, 4.0)
    order = jax.vmap(lambda own: jax.random.permutation(own, LEAF))(jax.random.split(seeds[3], DEVICES)).reshape((DEVICES, LEAF)).astype(jnp.int32)
    basis = centred(seeds[4], (POINTS, LEVELS, RANK), 1.0, 6.0, ((0, 256),))
    probes = centred(seeds[5], (PROBES, POINTS), 1.0, 8.0, ((1, 256),), jnp.float32)
    return {"coords": coords, "inv_length": inv_length, "noise": noise, "order": order, "basis": basis, "probes": probes}


GAMMA = 0.08
ROOT_OF_THREE = math.sqrt(3.0)

def leaf_kernel(input_locations, inv_length):
    scaled_distance = input_locations * inv_length[:, None]
    square = jnp.zeros((input_locations.shape[1], input_locations.shape[1]), jnp.float32)
    for comp in range(3):
        diff = scaled_distance[comp][:, None] - scaled_distance[comp][None, :]
        square = square + diff * diff
    dist = jnp.sqrt(square)
    return (1.0 + ROOT_OF_THREE * dist) * jnp.exp(-ROOT_OF_THREE * dist)

def reference(coords, inv_length, noise, order, basis, probes):
    leaves = order.shape[0]
    leaf = order.shape[1]
    total = leaves * leaf
    levels = basis.shape[1]
    rank = basis.shape[2]
    count = probes.shape[0]
    base = (jnp.arange(leaves, dtype=jnp.int32) * leaf)[:, None]
    index = (order.astype(jnp.int32) + base).reshape(-1)
    tree_coords = coords[:, index]
    tree_noise = noise[index]
    leaf_points = tree_coords.reshape(3, leaves, leaf).transpose(1, 0, 2)

    def operate(vector):
        blocks = vector.reshape(count, leaves, leaf).transpose(1, 0, 2)

        def one_leaf(item):
            kernel = leaf_kernel(item[0], inv_length)
            return jnp.dot(item[1], kernel, precision=lax.Precision.HIGHEST)
        near = lax.map(one_leaf, (leaf_points, blocks)).transpose(1, 0, 2).reshape(count, total)
        near = near + tree_noise[None, :] * vector
        rounded_values = vector.astype(jnp.bfloat16).astype(jnp.float32)
        far = jnp.zeros((count, total), jnp.float32)
        for level in range(levels):
            width = leaf * 2 ** level
            nodes = total // width
            left_factor_basis = basis[:, level, :].astype(jnp.float32).reshape(nodes, width, rank)
            right_factor_basis = rounded_values.reshape(count, nodes, width)
            kernel_factor = jnp.einsum('nek,ekh->enh', right_factor_basis, left_factor_basis, precision=lax.Precision.HIGHEST)
            swapped = kernel_factor.reshape(nodes // 2, 2, count, rank)[:, ::-1].reshape(nodes, count, rank)
            scaled_distance = (swapped * (GAMMA / width)).astype(jnp.bfloat16)
            scaled_distance = lax.optimization_barrier(scaled_distance).astype(jnp.float32)
            part = jnp.einsum('dtc,dsc->tds', scaled_distance, left_factor_basis, precision=lax.Precision.HIGHEST)
            far = far + part.reshape(count, total)
        return near + far
    solution = jnp.zeros_like(probes)
    residual = probes
    direction = probes
    norm_now = lax.optimization_barrier(jnp.sum(residual * residual, axis=1))
    for step in range(ITERS):
        image = operate(direction)
        alpha = norm_now / lax.optimization_barrier(jnp.sum(direction * image, axis=1))
        solution = solution + alpha[:, None] * direction
        residual = residual - alpha[:, None] * image
        norm_next = lax.optimization_barrier(jnp.sum(residual * residual, axis=1))
        direction = residual + (norm_next / norm_now)[:, None] * direction
        norm_now = norm_next
    return (solution, residual)
```

```python
import functools
import math

import jax
import jax.numpy as jnp
from jax import lax
from jax.experimental import pallas as pl
from jax.experimental.pallas import tpu as pltpu
from jax.sharding import PartitionSpec as P

GAMMA = 0.08
ROOT_OF_THREE = math.sqrt(3.0)
LEVELS = 8
RANK = 256
LEAF = 1024
PROBES = 128
PART = PROBES // 4
LANES = 128
F32 = jnp.float32
BF16 = jnp.bfloat16
VMEM_LIMIT = 48 * 2**20


def factor(level):
    return GAMMA / (LEAF * 2.0**level)


def call(kernel, out_shape, *args, scratch=(), smem=0, flops=0):
    specs = [pl.BlockSpec(memory_space=pltpu.SMEM)] * smem
    specs += [pl.BlockSpec(memory_space=pltpu.VMEM)] * (len(args) - smem)
    return pl.pallas_call(
        kernel,
        out_shape=out_shape,
        in_specs=specs,
        out_specs=jax.tree.map(
            lambda _: pl.BlockSpec(memory_space=pltpu.VMEM), out_shape
        ),
        scratch_shapes=list(scratch),
        compiler_params=pltpu.CompilerParams(vmem_limit_bytes=VMEM_LIMIT),
        cost_estimate=pl.CostEstimate(
            flops=flops, bytes_accessed=2**20, transcendentals=0
        ),
    )(*args)


def shape(*dims, dtype=F32):
    return jax.ShapeDtypeStruct(dims, dtype)


def dot(a, b):
    return jnp.dot(a, b, preferred_element_type=F32)


def dot_t(a, b):
    return lax.dot_general(a, b, (((1,), (1,)), ((), ())), preferred_element_type=F32)


def split(x):
    high = x.astype(BF16)
    return high, (x - high.astype(F32)).astype(BF16)


def near_product(v, high_ref, low_ref):
    v_high, v_low = split(v)
    return (
        dot(v_low, high_ref[...]) + dot(v_high, low_ref[...]) + dot(v_high, high_ref[...])
    )


def hand_out(y, full_ref, part_refs):
    for k, part_ref in enumerate(part_refs):
        part_ref[...] = full_ref[pl.ds(pl.multiple_of((y ^ k) * PART, PART), PART), :]


def coefficients_kernel(y_ref, v_ref, basis_ref, *rest):
    parts, full = rest[:4], rest[4]
    v = v_ref[...].astype(BF16)
    for level in range(LEVELS):
        full[:, level * RANK : (level + 1) * RANK] = dot(v, basis_ref[level])
    hand_out(y_ref[0], full, parts)


def kernel_matrix_kernel(rows_ref, cols_ref, noise_ref, v_ref, near_ref, high_ref, low_ref):
    step = 128

    @pl.loop(0, LEAF // step)
    def _(i):
        at = pl.ds(pl.multiple_of(i * step, step), step)
        square = jnp.zeros((step, LEAF), F32)
        for c in range(3):
            diff = cols_ref[at, c : c + 1] - rows_ref[c : c + 1, :]
            square = square + diff * diff
        t = ROOT_OF_THREE * jnp.sqrt(square)
        value = (1.0 + t) * jnp.exp(-t)
        high, low = split(value)
        high_ref[at, :] = high
        low_ref[at, :] = low

    v = v_ref[...]
    near_ref[...] = near_product(v, high_ref, low_ref) + noise_ref[...] * v


def gather_far(y, back_refs, sib_ref, basis_ref):
    for k, back_ref in enumerate(back_refs):
        at = pl.ds(pl.multiple_of((y ^ k) * PART, PART), PART)
        for level in range(LEVELS):
            lanes = slice(level * RANK, (level + 1) * RANK)
            sib_ref[at, lanes] = (back_ref[:, lanes] * factor(level)).astype(BF16)
    far = dot_t(sib_ref[:, :RANK], basis_ref[0])
    for level in range(1, LEVELS):
        far += dot_t(sib_ref[:, level * RANK : (level + 1) * RANK], basis_ref[level])
    return far


def image_kernel(y_ref, *refs):
    backs = refs[:4]
    basis_ref, near_ref, v_ref, high_ref, low_ref, noise_ref = refs[4:10]
    parts = refs[10:14]
    image_ref, next_near_ref, sib_ref, full = refs[14:]
    y = y_ref[0]
    image = near_ref[...] + gather_far(y, backs, sib_ref, basis_ref)
    image_ref[...] = image
    rounded = image.astype(BF16)
    for level in range(LEVELS):
        full[:, level * RANK : (level + 1) * RANK] = dot(rounded, basis_ref[level])
    next_near = near_product(image, high_ref, low_ref) + noise_ref[...] * image
    next_near_ref[...] = next_near
    v = v_ref[...]
    lane = lax.broadcasted_iota(jnp.int32, (PROBES, LANES), 1)
    block = jnp.zeros((PROBES, LANES), F32)
    for i, term in enumerate((v * v, v * image, image * image, image * next_near)):
        block = jnp.where(lane == i, jnp.sum(term, axis=1, keepdims=True), block)
    full[:, LEVELS * RANK :] = block
    hand_out(y, full, parts)


def final_kernel(y_ref, *refs):
    backs = refs[:4]
    basis_ref, near_ref, image_ref, v_ref, x_ref, r_ref, sib_ref, dots = refs[4:]
    y = y_ref[0]
    for k, back_ref in enumerate(backs):
        at = pl.ds(pl.multiple_of((y ^ k) * PART, PART), PART)
        dots[at, :] = back_ref[:, LEVELS * RANK :]
    second = near_ref[...] + gather_far(y, backs, sib_ref, basis_ref)
    m0, m1, m2, m3 = (dots[:, i : i + 1] for i in range(4))
    alpha = m0 / m1
    ratio = m2 / m1
    norm = alpha * alpha * m2 - m0
    curve = alpha * alpha * (m3 - ratio * m2)
    alpha_next = norm / curve
    grown = alpha * ratio
    v = v_ref[...]
    image = image_ref[...]
    x_ref[...] = alpha * v + alpha_next * (grown * v - alpha * image)
    r_ref[...] = v - alpha * image - alpha_next * (grown * image - alpha * second)


def pair_dot(a, b, level):
    return 2.0 * factor(level) * jnp.sum(a * b, axis=1, keepdims=True)


def third(x):
    lane = lax.broadcasted_iota(jnp.int32, (PART, LANES), 1)
    return jnp.where(lane == 3, x, 0.0)


def low_kernel(dots, r0, r1, r2, r3, total_ref):
    start = 2 * RANK
    total_ref[...] = (r0[:, start:] + r1[:, start:]) + (r2[:, start:] + r3[:, start:])
    if dots:
        a, b = slice(0, RANK), slice(RANK, 2 * RANK)
        term = pair_dot(r0[:, a], r1[:, a], 0) + pair_dot(r2[:, a], r3[:, a], 0)
        term += pair_dot(r0[:, b] + r1[:, b], r2[:, b] + r3[:, b], 1)
        total_ref[:, -LANES:] += third(term)


def step_kernel(dots, level, own, other, total_ref):
    total_ref[...] = own[:, RANK:] + other[:, RANK:]
    if dots:
        total_ref[:, -LANES:] += third(pair_dot(own[:, :RANK], other[:, :RANK], level))


def back_kernel(dots, *refs):
    r, sibs = refs[:4], refs[4:10]
    outs = refs[10:] if not dots else refs[11:]
    for k in range(4):
        outs[k][:, :RANK] = r[k ^ 1][:, :RANK]
        outs[k][:, RANK : 2 * RANK] = (
            r[k ^ 2][:, RANK : 2 * RANK] + r[k ^ 3][:, RANK : 2 * RANK]
        )
        for level in range(2, LEVELS):
            lanes = slice(level * RANK, (level + 1) * RANK)
            outs[k][:, lanes] = sibs[level - 2][:, :RANK]
        if dots:
            outs[k][:, LEVELS * RANK :] = refs[10][...]


def swap(x, axis, mask):
    return lax.ppermute(x, axis, [(i, i ^ mask) for i in range(lax.axis_size(axis))])


HOPS = (("local", 4), ("local", 8), ("local", 24), ("group", 1), ("group", 2), ("group", 6))


def exchange(parts, dots):
    extra = LANES if dots else 0
    moved = [parts[0]] + [swap(parts[k], "local", k) for k in (1, 2, 3)]
    total = call(
        functools.partial(low_kernel, dots),
        shape(PART, (LEVELS - 2) * RANK + extra),
        *moved,
    )
    sibs = []
    for level, (axis, mask) in enumerate(HOPS, 2):
        other = swap(total, axis, mask)
        sibs.append(other)
        width = (LEVELS - 1 - level) * RANK + extra
        if width:
            total = call(
                functools.partial(step_kernel, dots, level),
                shape(PART, width),
                total,
                other,
            )
    outs = call(
        functools.partial(back_kernel, dots),
        (shape(PART, LEVELS * RANK + extra),) * 4,
        *moved,
        *sibs,
        *([total] if dots else []),
    )
    return [outs[0]] + [swap(outs[k], "local", k) for k in (1, 2, 3)]


def per_device(coords, inv_length, noise, order, basis, probes):
    index = order[0]
    scaled = jnp.take(coords, index, axis=1) * inv_length[:, None]
    tree_noise = jnp.take(noise, index, axis=0)[None, :]
    y = (lax.axis_index("local") & 3).astype(jnp.int32)[None]
    levels_first = jnp.transpose(basis, (1, 0, 2))
    full = LEVELS * RANK
    parts = call(
        coefficients_kernel,
        (shape(PART, full),) * 4,
        y,
        probes,
        levels_first,
        scratch=[pltpu.VMEM((PROBES, full), F32)],
        smem=1,
        flops=2 * PROBES * LEAF * full,
    )
    square = shape(LEAF, LEAF, dtype=BF16)
    vectors = shape(PROBES, LEAF)
    near, high, low = call(
        kernel_matrix_kernel,
        (vectors, square, square),
        scaled,
        scaled.T,
        tree_noise,
        probes,
        flops=6 * PROBES * LEAF * LEAF,
    )
    backs = exchange(parts, False)
    *parts, image, near = call(
        image_kernel,
        (shape(PART, full + LANES),) * 4 + (vectors, vectors),
        y,
        *backs,
        levels_first,
        near,
        probes,
        high,
        low,
        tree_noise,
        scratch=[pltpu.VMEM((PROBES, full), BF16), pltpu.VMEM((PROBES, full + LANES), F32)],
        smem=1,
        flops=4 * PROBES * LEAF * full,
    )
    backs = exchange(parts, True)
    return call(
        final_kernel,
        (vectors, vectors),
        y,
        *backs,
        levels_first,
        near,
        image,
        probes,
        scratch=[pltpu.VMEM((PROBES, full), BF16), pltpu.VMEM((PROBES, LANES), F32)],
        smem=1,
        flops=2 * PROBES * LEAF * full,
    )


def solution(mesh):
    in_specs = (
        P(None, ("group", "local")),
        P(),
        P(("group", "local")),
        P(("group", "local"), None),
        P(("group", "local"), None, None),
        P(None, ("group", "local")),
    )
    out_specs = (P(None, ("group", "local")), P(None, ("group", "local")))
    return jax.shard_map(
        per_device, mesh=mesh, in_specs=in_specs, out_specs=out_specs, check_vma=False
    )
```

```python
import functools
import math

import jax
import jax.numpy as jnp
from jax import lax
from jax.experimental import pallas as pl
from jax.experimental.pallas import tpu as pltpu
from jax.sharding import PartitionSpec as P

GAMMA = 0.08
ROOT_OF_THREE = math.sqrt(3.0)
LEVELS = 8
RANK = 256
LEAF = 1024
PROBES = 128
PART = PROBES // 4
ROWS = PART // 2
LANES = 128
CHUNKS = 8
START_LIMIT = 52
F32 = jnp.float32
BF16 = jnp.bfloat16
VMEM = pl.BlockSpec(memory_space=pltpu.VMEM)
SMEM = pl.BlockSpec(memory_space=pltpu.SMEM)
ANY = pl.BlockSpec(memory_space=pl.ANY)
HBM = pl.BlockSpec(memory_space=pltpu.HBM)


def factor(level):
    return GAMMA / (LEAF * 2.0**level)


def call(kernel, out_shape, *args, scratch=(), smem=0, anywhere=0, outside=0, flops=0, limit=16, outs=None):
    held = len(args) - smem - anywhere - outside
    return pl.pallas_call(
        kernel,
        out_shape=out_shape,
        in_specs=[SMEM] * smem + [VMEM] * held + [ANY] * anywhere + [HBM] * outside,
        out_specs=outs or jax.tree.map(lambda _: VMEM, out_shape),
        scratch_shapes=list(scratch),
        compiler_params=pltpu.CompilerParams(vmem_limit_bytes=limit * 2**20),
        cost_estimate=pl.CostEstimate(
            flops=flops, bytes_accessed=2**20, transcendentals=0
        ),
    )(*args)


def shape(*dims, dtype=F32):
    return jax.ShapeDtypeStruct(dims, dtype)


def dot(a, b):
    return jnp.dot(a, b, preferred_element_type=F32)


def dot_t(a, b):
    return lax.dot_general(a, b, (((1,), (1,)), ((), ())), preferred_element_type=F32)


def split(x):
    high = x.astype(BF16)
    return high, (x - high.astype(F32)).astype(BF16)


def level_lanes(i):
    return slice(i * RANK, (i + 1) * RANK)


def owned(i, core):
    return pl.ds(pl.multiple_of(i * PART + core * ROWS, ROWS), ROWS)


def quarter(y, k):
    return pl.ds(pl.multiple_of((y ^ k) * PART, PART), PART)


def coefficients(v, basis_ref, levels, full_ref):
    for i, level in enumerate(levels):
        full_ref[:, level_lanes(i)] = dot(v, basis_ref[level])


def own_half(core):
    return pl.ds(pl.multiple_of(core * LANES, LANES), LANES)


def scatter_halves(core, full_ref, send_ref, keep_ref, at):
    for i in range(2):
        lanes = slice(i * LANES, (i + 1) * LANES)
        half = full_ref.at[:, level_lanes(i)]
        keep_ref[:, lanes] = half[:, own_half(core)]
        send_ref[:, at + i * LANES : at + (i + 1) * LANES] = half[:, own_half(1 - core)]


def start_kernel(core_ref, v_hbm, flat_ref, basis_out, send_ref, keep_ref, low_ref, full, held, basis_ref, v_ref, sems):
    rows = LEAF * LEVELS // CHUNKS
    points = LEAF // CHUNKS
    copies = [
        pltpu.make_async_copy(
            flat_ref.at[pl.ds(i * rows, rows)], held.at[pl.ds(i * rows, rows)], sems.at[i]
        )
        for i in range(CHUNKS)
    ]
    saves = [
        pltpu.make_async_copy(
            basis_ref.at[:, pl.ds(i * points, points)],
            basis_out.at[:, pl.ds(i * points, points)],
            sems.at[CHUNKS + 1 + i],
        )
        for i in range(CHUNKS)
    ]
    last = pltpu.make_async_copy(v_hbm, v_ref, sems.at[CHUNKS])
    for copy in copies:
        copy.start()
    last.start()
    width = 32
    block = width * LEVELS
    to = lax.broadcasted_iota(jnp.int32, (block, block), 0)
    at = lax.broadcasted_iota(jnp.int32, (block, block), 1)
    source = (to & (width - 1)) * LEVELS + (to >> 5)
    order = jnp.where(at == source, 1.0, 0.0).astype(BF16)
    for i, copy in enumerate(copies):
        copy.wait()
        for j in range(i * rows // block, (i + 1) * rows // block):
            moved = dot(order, held[j * block : (j + 1) * block, :]).astype(BF16)
            for level in range(LEVELS):
                basis_ref[level, j * width : (j + 1) * width, :] = moved[
                    level * width : (level + 1) * width
                ]
        saves[i].start()
    last.wait()
    v = v_ref[...].astype(BF16)
    send_ref[:, :RANK] = dot(v, basis_ref[5])
    coefficients(v, basis_ref, (6, 7), full)
    scatter_halves(core_ref[0], full, send_ref, keep_ref, RANK)
    coefficients(v, basis_ref, (2, 3, 4), low_ref)
    for save in saves:
        save.wait()


def whole_kernel(levels, v_ref, basis_ref, gate_ref, out_ref):
    coefficients(v_ref[...].astype(BF16), basis_ref, levels, out_ref)


def parts_kernel(y_ref, low_ref, keep_ref, other_ref, *parts):
    for k, part in enumerate(parts):
        at = quarter(y_ref[0], k)
        part[:, : 3 * RANK] = low_ref[at, :]
        part[:, 3 * RANK : 4 * RANK] = other_ref[at, :RANK]
        part[:, 4 * RANK :] = keep_ref[at, :] + other_ref[at, RANK:]


def gather_kernel(order_ref, values_ref, gate_ref, out_ref):
    x = values_ref[...]
    a, rest = x.astype(BF16), x - x.astype(BF16).astype(F32)
    b, c = split(rest)
    pieces = jnp.concatenate([a, b, c], axis=0)
    step = 256
    total = None
    for i in range(LEAF // step):
        source = lax.broadcasted_iota(jnp.int32, (step, LEAF), 0) + i * step
        hot = jnp.where(source == order_ref[...], 1.0, 0.0).astype(BF16)
        term = dot(pieces[:, i * step : (i + 1) * step], hot)
        total = term if total is None else total + term
    out_ref[...] = total[:8] + total[8:16] + total[16:]


def matrix_kernel(half, values_ref, high_ref, low_ref):
    step = 128
    columns = values_ref[...].T
    for i in range(LEAF // 2 // step):
        at = slice(half * LEAF // 2 + i * step, half * LEAF // 2 + (i + 1) * step)
        square = None
        for c in range(3):
            diff = columns[at, c : c + 1] - values_ref[c : c + 1, :]
            square = diff * diff if square is None else square + diff * diff
        t = ROOT_OF_THREE * jnp.sqrt(square)
        high, low = split((1.0 + t) * jnp.exp(-t))
        high_ref[i * step : (i + 1) * step, :] = high
        low_ref[i * step : (i + 1) * step, :] = low


def near_kernel(v_ref, values_ref, high0, high1, low0, low1, *rest):
    out_ref = rest[-1]
    v = v_ref[...]
    v_high, v_low = split(v)
    both = LEAF // 2
    first, second = slice(0, both), slice(both, LEAF)
    out_ref[...] = (
        (dot(v_low[:, first], high0[...]) + dot(v_low[:, second], high1[...]))
        + (dot(v_high[:, first], low0[...]) + dot(v_high[:, second], low1[...]))
        + (dot(v_high[:, first], high0[...]) + dot(v_high[:, second], high1[...]))
        + values_ref[3:4, :] * v
    )


def base_kernel(near_ref, basis_ref, sib0, sib1, out_ref):
    zero = (sib0[:, :RANK] * factor(0)).astype(BF16)
    one = (sib1[...] * factor(1)).astype(BF16)
    out_ref[...] = (
        near_ref[...] + dot_t(zero, basis_ref[0]) + dot_t(one, basis_ref[1])
    )


def far_first_kernel(y_ref, basis_ref, b0, b1, b2, b3, out_ref, held):
    for k, back in enumerate((b0, b1, b2, b3)):
        for i in range(4):
            held[quarter(y_ref[0], k), level_lanes(i)] = (
                back[:, level_lanes(i)] * factor(2 + i)
            ).astype(BF16)
    total = None
    for i in range(4):
        term = dot_t(held[:, level_lanes(i)], basis_ref[2 + i])
        total = term if total is None else total + term
    out_ref[...] = total


def far_of_halves(core, own_ref, other_ref, levels, basis_ref, held, total):
    for i in range(len(levels)):
        for ref, side in ((own_ref, core), (other_ref, 1 - core)):
            scaled = (ref[:, level_lanes(i)] * factor(levels[i])).astype(BF16)
            for j in range(4):
                held[owned(j, side), level_lanes(i)] = scaled[j * ROWS : (j + 1) * ROWS]
    for i, level in enumerate(levels):
        total += dot_t(held[:, level_lanes(i)], basis_ref[level])
    return total


def far_second_kernel(core_ref, near_ref, basis_ref, own_ref, other_ref, out_ref, held):
    out_ref[...] = far_of_halves(
        core_ref[0], own_ref, other_ref, (0, 1, 2), basis_ref, held, near_ref[...]
    )


def far_high(core, own_ref, other_ref, basis_ref, held):
    for i in range(2):
        lanes = slice(i * LANES, (i + 1) * LANES)
        half = held.at[:, level_lanes(i)]
        half[:, own_half(core)] = (own_ref[:, lanes] * factor(6 + i)).astype(BF16)
        half[:, own_half(1 - core)] = (other_ref[:, lanes] * factor(6 + i)).astype(BF16)
    return dot_t(held[:, level_lanes(0)], basis_ref[6]) + dot_t(
        held[:, level_lanes(1)], basis_ref[7]
    )


def middle_kernel(core_ref, own_ref, other_ref, *refs):
    core = core_ref[0]
    basis_ref, base_ref, far_ref, near_ref, v_ref, values_ref, high0, high1 = refs[:8]
    image_ref, send_ref, keep_ref, held, full = refs[8:]
    far = far_ref[...] + far_high(core, own_ref, other_ref, basis_ref, held)
    base = base_ref[...]
    image = base + far
    image_ref[...] = image
    coefficients(image.astype(BF16), basis_ref, range(LEVELS), full)
    near = near_ref[...]
    rounded = far.astype(BF16)
    half = LEAF // 2
    own = (
        dot(rounded[:, :half], high0[...])
        + dot(rounded[:, half:], high1[...])
        + values_ref[3:4, :] * far
    )
    v = v_ref[...]
    curve = base * near + far * (2.0 * near + own)
    lane = lax.broadcasted_iota(jnp.int32, (PROBES, LANES), 1)
    block = jnp.zeros((PROBES, LANES), F32)
    for i, term in enumerate((v * v, v * image, image * image, curve)):
        block = jnp.where(lane == i, jnp.sum(term, axis=1, keepdims=True), block)
    full[:, LEVELS * RANK :] = block
    for i in range(4):
        to = slice(i * ROWS, (i + 1) * ROWS)
        send_ref[to, :] = full[owned(i, 1 - core), :]
        keep_ref[to, :] = full[owned(i, core), :]


def final_kernel(core_ref, own_ref, other_ref, basis_ref, low_ref, image_ref, v_ref, x_ref, r_ref, held, dots):
    core = core_ref[0]
    for ref, side in ((own_ref, core), (other_ref, 1 - core)):
        for j in range(4):
            dots[owned(j, side), :] = ref[j * ROWS : (j + 1) * ROWS, 5 * RANK :]
    second = far_of_halves(
        core, own_ref, other_ref, (3, 4, 5, 6, 7), basis_ref, held, low_ref[...]
    )
    m0, m1, m2, m3 = (dots[:, i : i + 1] for i in range(4))
    alpha = m0 / m1
    ratio = m2 / m1
    norm = alpha * alpha * m2 - m0
    curve = alpha * alpha * (m3 - ratio * m2)
    alpha_next = norm / curve
    grown = alpha * ratio
    v = v_ref[...]
    image = image_ref[...]
    x_ref[...] = alpha * v + alpha_next * (grown * v - alpha * image)
    r_ref[...] = v - alpha * image - alpha_next * (grown * image - alpha * second)


def assemble_kernel(y_ref, b0, b1, b2, b3, out_ref):
    for k, back in enumerate((b0, b1, b2, b3)):
        out_ref[quarter(y_ref[0], k), :] = back[:, 4 * RANK :]


def pair_dot(a, b, level):
    return 2.0 * factor(level) * jnp.sum(a * b, axis=1, keepdims=True)


def in_lane(i, x):
    lane = lax.broadcasted_iota(jnp.int32, (PART, LANES), 1)
    return jnp.where(lane == i, x, 0.0)


def sum_kernel(r0, r1, r2, r3, gate_ref, total_ref):
    total_ref[...] = (r0[...] + r1[...]) + (r2[...] + r3[...])


def shift_kernel(own, other, out_ref):
    out_ref[...] = own[:, RANK:] + other[:, RANK:]


def six_seven_kernel(own, other, *refs):
    six_ref, seven_ref = refs[-2:]
    six, seven = slice(2 * RANK, 2 * RANK + LANES), slice(2 * RANK + LANES, 3 * RANK)
    six_ref[...] = own[:, six] + other[:, six]
    seven_ref[...] = own[:, seven] + other[:, seven]


def join_first_kernel(two, three, four, own, x1, x2, x3, gate_ref, out_ref):
    out_ref[:, level_lanes(0)] = two[:, :RANK]
    out_ref[:, level_lanes(1)] = three[:, :RANK]
    out_ref[:, level_lanes(2)] = four[:, :RANK]
    out_ref[:, level_lanes(3)] = own[:, level_lanes(1)] + four[:, level_lanes(1)]
    out_ref[:, 4 * RANK : 4 * RANK + LANES] = x1[...]
    out_ref[:, 4 * RANK + LANES :] = x2[...] + x3[...]


def merge_kernel(y_ref, keep_ref, other_ref, *parts):
    end = 6 * RANK
    for k, part_ref in enumerate(parts):
        at = pl.ds(pl.multiple_of((y_ref[0] ^ k) * ROWS, ROWS), ROWS)
        for level in range(6):
            part_ref[:, level_lanes(2 * level)] = keep_ref[at, level_lanes(level)]
            part_ref[:, level_lanes(2 * level + 1)] = other_ref[at, level_lanes(level)]
        part_ref[:, 2 * end :] = keep_ref[at, end:] + other_ref[at, end:]


def add_dot(total_ref, lane, term):
    lanes = lax.broadcasted_iota(jnp.int32, (ROWS, LANES), 1)
    total_ref[:, -LANES:] += jnp.where(lanes == lane, term, 0.0)


def y_dots_kernel(r0, r1, r2, r3, gate_ref, total_ref):
    pair = 2 * RANK
    start = 2 * pair
    total_ref[...] = (r0[:, start:] + r1[:, start:]) + (r2[:, start:] + r3[:, start:])
    a, b = slice(0, pair), slice(pair, start)
    term = pair_dot(r0[:, a], r1[:, a], 0) + pair_dot(r2[:, a], r3[:, a], 0)
    term += pair_dot(r0[:, b] + r1[:, b], r2[:, b] + r3[:, b], 1)
    add_dot(total_ref, 3, term)


def step_kernel(level, own, other, *rest):
    total_ref = rest[-1]
    pair = 2 * RANK
    total_ref[...] = own[:, pair:] + other[:, pair:]
    add_dot(total_ref, 3, pair_dot(own[:, :pair], other[:, :pair], level))


def core_dots_kernel(own, total_ref):
    total_ref[...] = own[:, 2 * RANK :]
    add_dot(total_ref, 3, pair_dot(own[:, level_lanes(0)], own[:, level_lanes(1)], 5))


def low_join_kernel(r0, r1, r2, r3, two, gate_ref, *outs):
    r = (r0, r1, r2, r3)
    pair = 2 * RANK
    zero, one = slice(0, pair), slice(pair, 2 * pair)
    for k, out in enumerate(outs):
        out[:, zero] = r[k ^ 1][:, zero]
        out[:, one] = r[k ^ 2][:, one] + r[k ^ 3][:, one]
        out[:, 2 * pair :] = two[:, :pair]


def high_join_kernel(three, four, five, own, x1, x2, x3, out_ref):
    a, b, q = slice(0, RANK), slice(RANK, 2 * RANK), slice(2 * RANK, 2 * RANK + LANES)
    far = x2[:, b] + x3[:, b]
    pair = 2 * RANK
    out_ref[:, :pair] = three[:, :pair]
    out_ref[:, pair : 2 * pair] = four[:, :pair]
    out_ref[:, level_lanes(4)] = five[:, level_lanes(1)]
    out_ref[:, level_lanes(5)] = five[:, level_lanes(0)]
    out_ref[:, level_lanes(6)] = x1[:, a]
    out_ref[:, level_lanes(7)] = far
    out_ref[:, 8 * RANK :] = (own[:, q] + x1[:, q]) + (x2[:, q] + x3[:, q])
    term = pair_dot(own[:, a], x1[:, a], 6) + pair_dot(x2[:, a], x3[:, a], 6)
    term += pair_dot(own[:, b] + x1[:, b], far, 7)
    add_dot(out_ref, 3, term)


def gather_kernel_of(levels, shared, y_ref, b0, b1, b2, b3, *rest):
    own_ref, send_ref = rest[-2:]
    for k, back in enumerate((b0, b1, b2, b3)):
        at = pl.ds(pl.multiple_of((y_ref[0] ^ k) * ROWS, ROWS), ROWS)
        for i in range(levels):
            own_ref[at, level_lanes(i)] = back[:, level_lanes(2 * i)]
            send_ref[at, level_lanes(i)] = back[:, level_lanes(2 * i + 1)]
        if shared:
            own_ref[at, levels * RANK :] = back[:, 2 * levels * RANK :]
            send_ref[at, levels * RANK :] = back[:, 2 * levels * RANK :]


def swap(x, axis, mask):
    return lax.ppermute(x, axis, [(i, i ^ mask) for i in range(lax.axis_size(axis))])


def over_y(x):
    return [x[0]] + [swap(x[k], "local", k) for k in (1, 2, 3)]


Z1, Z2, Z3 = ("local", 4), ("local", 8), ("local", 24)
CORE, X1, X2, X3 = ("group", 1), ("group", 2), ("group", 4), ("group", 6)


def rows(lanes):
    return shape(ROWS, lanes)


def part(lanes):
    return shape(PART, lanes)


def per_device(coords, inv_length, noise, order, basis, probes):
    y = (lax.axis_index("local") & 3).astype(jnp.int32)[None]
    core = (lax.axis_index("group") & 1).astype(jnp.int32)[None]
    flat = basis.reshape(LEAF * LEVELS, RANK)
    square = shape(LEAF // 2, LEAF, dtype=BF16)
    vectors = shape(PROBES, LEAF)
    both = shape(PROBES, RANK)

    basis, send, keep, low = call(
        start_kernel,
        (
            shape(LEVELS, LEAF, RANK, dtype=BF16),
            shape(PROBES, 2 * RANK),
            both,
            shape(PROBES, 3 * RANK),
        ),
        core,
        probes,
        flat,
        scratch=[
            pltpu.VMEM((PROBES, 2 * RANK), F32),
            pltpu.VMEM((LEAF * LEVELS, RANK), BF16),
            pltpu.VMEM((LEVELS, LEAF, RANK), BF16),
            pltpu.VMEM((PROBES, LEAF), F32),
            pltpu.SemaphoreType.DMA((2 * CHUNKS + 1,)),
        ],
        smem=1,
        outside=2,
        flops=2**31,
        limit=START_LIMIT,
        outs=(ANY, VMEM, VMEM, VMEM),
    )
    other = swap(send, *CORE)
    parts = call(parts_kernel, (part(5 * RANK),) * 4, y, low, keep, other, smem=1)
    moved = over_y(parts)

    values = jnp.concatenate(
        [coords * inv_length[:, None], noise[None, :], jnp.zeros((4, LEAF), F32)], axis=0
    )
    values = call(
        gather_kernel, shape(8, LEAF), order, values, parts[0], anywhere=1, flops=2**26
    )
    high0, low0 = call(
        functools.partial(matrix_kernel, 0), (square, square), values, flops=2**30
    )
    high1, low1 = call(
        functools.partial(matrix_kernel, 1), (square, square), values, flops=2**30
    )
    matrix = (values, high0, high1, low0, low1)
    near = call(near_kernel, vectors, probes, *matrix, flops=2**30)

    total = call(sum_kernel, part(5 * RANK), *moved, near, anywhere=1)
    two = swap(total, *Z1)
    leaf = call(
        functools.partial(whole_kernel, (0, 1)),
        shape(PROBES, 2 * RANK),
        probes,
        basis,
        total,
        anywhere=1,
        flops=2**28,
    )
    leaf_other = swap(leaf, "local", 1)
    total = call(shift_kernel, part(4 * RANK), total, two)
    three = swap(total, *Z2)
    leaf_next = call(shift_kernel, both, leaf, leaf_other)
    one = swap(leaf_next, "local", 3)
    total = call(shift_kernel, part(3 * RANK), total, three)
    four = swap(total, *Z3)
    six, seven = call(
        six_seven_kernel, (part(LANES),) * 2, total, four, one, anywhere=1
    )
    x1, x2, x3 = swap(six, *X1), swap(seven, *X2), swap(seven, *X3)
    base = call(base_kernel, vectors, near, basis, leaf_other, one, flops=2**28)
    base_near = call(near_kernel, vectors, base, *matrix, flops=2**30)
    back = call(
        join_first_kernel,
        part(5 * RANK),
        two,
        three,
        four,
        total,
        x1,
        x2,
        x3,
        base_near,
        anywhere=1,
    )
    back = over_y([back] * 4)
    own = call(assemble_kernel, both, y, *back, smem=1)
    other = swap(own, *CORE)
    far = call(
        far_first_kernel,
        vectors,
        y,
        basis,
        *back,
        scratch=[pltpu.VMEM((PROBES, 4 * RANK), BF16)],
        smem=1,
        flops=2**29,
    )
    wide = LEVELS * RANK + LANES
    image, send, keep = call(
        middle_kernel,
        (vectors, shape(PROBES // 2, wide), shape(PROBES // 2, wide)),
        core,
        own,
        other,
        basis,
        base,
        far,
        base_near,
        probes,
        values,
        high0,
        high1,
        scratch=[pltpu.VMEM((PROBES, 2 * RANK), BF16), pltpu.VMEM((PROBES, wide), F32)],
        smem=1,
        flops=2**30,
    )

    other = swap(send, *CORE)
    parts = call(merge_kernel, (rows(14 * RANK + LANES),) * 4, y, keep, other, smem=1)
    moved = over_y(parts)
    near = call(
        near_kernel, vectors, image, *matrix, parts[0], anywhere=1, flops=2**30
    )
    total = call(
        y_dots_kernel, rows(10 * RANK + LANES), *moved, near, anywhere=1
    )
    two = swap(total, *Z1)
    total = call(functools.partial(step_kernel, 2), rows(8 * RANK + LANES), total, two)
    three = swap(total, *Z2)
    back = call(low_join_kernel, (rows(6 * RANK),) * 4, *moved, two, total, anywhere=1)
    back = over_y(back)
    total = call(functools.partial(step_kernel, 3), rows(6 * RANK + LANES), total, three)
    four = swap(total, *Z3)
    five = call(
        functools.partial(step_kernel, 4),
        rows(4 * RANK + LANES),
        total,
        four,
        *back[1:],
        anywhere=3,
    )
    total = call(core_dots_kernel, rows(2 * RANK + LANES), five)
    x1, x2, x3 = swap(total, *X1), swap(total, *X2), swap(total, *X3)
    low_own, send = call(
        functools.partial(gather_kernel_of, 3, False),
        (shape(PROBES // 2, 3 * RANK),) * 2,
        y,
        *back,
        smem=1,
    )
    low_other = swap(send, *CORE)
    high_back = call(
        high_join_kernel, rows(8 * RANK + LANES), three, four, five, total, x1, x2, x3
    )
    high_back = over_y([high_back] * 4)
    partial_second = call(
        far_second_kernel,
        vectors,
        core,
        near,
        basis,
        low_own,
        low_other,
        scratch=[pltpu.VMEM((PROBES, 3 * RANK), BF16)],
        smem=1,
        flops=2**29,
    )
    own, send = call(
        functools.partial(gather_kernel_of, 3, True),
        (shape(PROBES // 2, 5 * RANK + LANES),) * 2,
        y,
        *high_back,
        partial_second,
        smem=1,
        anywhere=1,
    )
    other = swap(send, *CORE)
    return call(
        final_kernel,
        (vectors, vectors),
        core,
        own,
        other,
        basis,
        partial_second,
        image,
        probes,
        scratch=[pltpu.VMEM((PROBES, 5 * RANK), BF16), pltpu.VMEM((PROBES, LANES), F32)],
        smem=1,
        flops=2**29,
    )


def solution(mesh):
    in_specs = (
        P(None, ("group", "local")),
        P(),
        P(("group", "local")),
        P(("group", "local"), None),
        P(("group", "local"), None, None),
        P(None, ("group", "local")),
    )
    out_specs = (P(None, ("group", "local")), P(None, ("group", "local")))
    return jax.shard_map(
        per_device, mesh=mesh, in_specs=in_specs, out_specs=out_specs, check_vma=False
    )
```

```python
import functools
import math

import jax
import jax.numpy as jnp
from jax import lax
from jax.experimental import pallas as pl
from jax.experimental.pallas import tpu as pltpu
from jax.sharding import PartitionSpec as P

GAMMA = 0.08
ROOT_OF_THREE = math.sqrt(3.0)
LEVELS = 8
RANK = 256
LEAF = 1024
PROBES = 128
PART = PROBES // 4
ROWS = PART // 2
LANES = 128
CHUNKS = 8
START_LIMIT = 52
F32 = jnp.float32
BF16 = jnp.bfloat16
VMEM = pl.BlockSpec(memory_space=pltpu.VMEM)
SMEM = pl.BlockSpec(memory_space=pltpu.SMEM)
ANY = pl.BlockSpec(memory_space=pl.ANY)
HBM = pl.BlockSpec(memory_space=pltpu.HBM)


def factor(level):
    return GAMMA / (LEAF * 2.0**level)


def call(kernel, out_shape, *args, scratch=(), smem=0, anywhere=0, outside=0, flops=0, limit=16, outs=None):
    held = len(args) - smem - anywhere - outside
    return pl.pallas_call(
        kernel,
        out_shape=out_shape,
        in_specs=[SMEM] * smem + [VMEM] * held + [ANY] * anywhere + [HBM] * outside,
        out_specs=outs or jax.tree.map(lambda _: VMEM, out_shape),
        scratch_shapes=list(scratch),
        compiler_params=pltpu.CompilerParams(vmem_limit_bytes=limit * 2**20),
        cost_estimate=pl.CostEstimate(
            flops=flops, bytes_accessed=2**20, transcendentals=0
        ),
    )(*args)


def shape(*dims, dtype=F32):
    return jax.ShapeDtypeStruct(dims, dtype)


def dot(a, b):
    return jnp.dot(a, b, preferred_element_type=F32)


def dot_t(a, b):
    return lax.dot_general(a, b, (((1,), (1,)), ((), ())), preferred_element_type=F32)


def split(x):
    high = x.astype(BF16)
    return high, (x - high.astype(F32)).astype(BF16)


def level_lanes(i):
    return slice(i * RANK, (i + 1) * RANK)


def owned(i, core):
    return pl.ds(pl.multiple_of(i * PART + core * ROWS, ROWS), ROWS)


def quarter(y, k):
    return pl.ds(pl.multiple_of((y ^ k) * PART, PART), PART)


def coefficients(v, basis_ref, levels, full_ref):
    for i, level in enumerate(levels):
        full_ref[:, level_lanes(i)] = dot(v, basis_ref[level])


def own_half(core):
    return pl.ds(pl.multiple_of(core * LANES, LANES), LANES)


def scatter_halves(core, full_ref, send_ref, keep_ref, at):
    for i in range(2):
        lanes = slice(i * LANES, (i + 1) * LANES)
        half = full_ref.at[:, level_lanes(i)]
        keep_ref[:, lanes] = half[:, own_half(core)]
        send_ref[:, at + i * LANES : at + (i + 1) * LANES] = half[:, own_half(1 - core)]


def start_kernel(core_ref, v_hbm, flat_ref, basis_out, send_ref, keep_ref, low_ref, full, held, basis_ref, v_ref, sems):
    rows = LEAF * LEVELS // CHUNKS
    points = LEAF // CHUNKS
    copies = [
        pltpu.make_async_copy(
            flat_ref.at[pl.ds(i * rows, rows)], held.at[pl.ds(i * rows, rows)], sems.at[i]
        )
        for i in range(CHUNKS)
    ]
    saves = [
        pltpu.make_async_copy(
            basis_ref.at[:, pl.ds(i * points, points)],
            basis_out.at[:, pl.ds(i * points, points)],
            sems.at[CHUNKS + 1 + i],
        )
        for i in range(CHUNKS)
    ]
    last = pltpu.make_async_copy(v_hbm, v_ref, sems.at[CHUNKS])
    for copy in copies:
        copy.start()
    last.start()
    width = 32
    block = width * LEVELS
    to = lax.broadcasted_iota(jnp.int32, (block, block), 0)
    at = lax.broadcasted_iota(jnp.int32, (block, block), 1)
    source = (to & (width - 1)) * LEVELS + (to >> 5)
    order = jnp.where(at == source, 1.0, 0.0).astype(BF16)
    for i, copy in enumerate(copies):
        copy.wait()
        for j in range(i * rows // block, (i + 1) * rows // block):
            moved = dot(order, held[j * block : (j + 1) * block, :]).astype(BF16)
            for level in range(LEVELS):
                basis_ref[level, j * width : (j + 1) * width, :] = moved[
                    level * width : (level + 1) * width
                ]
        saves[i].start()
    last.wait()
    v = v_ref[...].astype(BF16)
    send_ref[:, :RANK] = dot(v, basis_ref[5])
    coefficients(v, basis_ref, (6, 7), full)
    scatter_halves(core_ref[0], full, send_ref, keep_ref, RANK)
    coefficients(v, basis_ref, (2, 3, 4), low_ref)
    for save in saves:
        save.wait()


def whole_kernel(levels, v_ref, basis_ref, gate_ref, out_ref):
    coefficients(v_ref[...].astype(BF16), basis_ref, levels, out_ref)


def parts_kernel(y_ref, low_ref, keep_ref, other_ref, *parts):
    for k, part in enumerate(parts):
        at = quarter(y_ref[0], k)
        part[:, : 3 * RANK] = low_ref[at, :]
        part[:, 3 * RANK : 4 * RANK] = other_ref[at, :RANK]
        part[:, 4 * RANK :] = keep_ref[at, :] + other_ref[at, RANK:]


def gather_kernel(order_ref, values_ref, gate_ref, out_ref):
    x = values_ref[...]
    a, rest = x.astype(BF16), x - x.astype(BF16).astype(F32)
    b, c = split(rest)
    pieces = jnp.concatenate([a, b, c], axis=0)
    step = 256
    total = None
    for i in range(LEAF // step):
        source = lax.broadcasted_iota(jnp.int32, (step, LEAF), 0) + i * step
        hot = jnp.where(source == order_ref[...], 1.0, 0.0).astype(BF16)
        term = dot(pieces[:, i * step : (i + 1) * step], hot)
        total = term if total is None else total + term
    out_ref[...] = total[:8] + total[8:16] + total[16:]


def matrix_kernel(half, values_ref, high_ref, low_ref):
    step = 128
    columns = values_ref[...].T
    for i in range(LEAF // 2 // step):
        at = slice(half * LEAF // 2 + i * step, half * LEAF // 2 + (i + 1) * step)
        square = None
        for c in range(3):
            diff = columns[at, c : c + 1] - values_ref[c : c + 1, :]
            square = diff * diff if square is None else square + diff * diff
        t = ROOT_OF_THREE * jnp.sqrt(square)
        high, low = split((1.0 + t) * jnp.exp(-t))
        high_ref[i * step : (i + 1) * step, :] = high
        low_ref[i * step : (i + 1) * step, :] = low


def near_kernel(v_ref, values_ref, high0, high1, low0, low1, *rest):
    out_ref = rest[-1]
    v = v_ref[...]
    v_high, v_low = split(v)
    both = LEAF // 2
    first, second = slice(0, both), slice(both, LEAF)
    out_ref[...] = (
        (dot(v_low[:, first], high0[...]) + dot(v_low[:, second], high1[...]))
        + (dot(v_high[:, first], low0[...]) + dot(v_high[:, second], low1[...]))
        + (dot(v_high[:, first], high0[...]) + dot(v_high[:, second], high1[...]))
        + values_ref[3:4, :] * v
    )


def base_kernel(near_ref, basis_ref, sib0, sib1, out_ref):
    zero = (sib0[:, :RANK] * factor(0)).astype(BF16)
    one = (sib1[...] * factor(1)).astype(BF16)
    out_ref[...] = (
        near_ref[...] + dot_t(zero, basis_ref[0]) + dot_t(one, basis_ref[1])
    )


def far_first_kernel(y_ref, basis_ref, b0, b1, b2, b3, out_ref, held):
    for k, back in enumerate((b0, b1, b2, b3)):
        for i in range(4):
            held[quarter(y_ref[0], k), level_lanes(i)] = (
                back[:, level_lanes(i)] * factor(2 + i)
            ).astype(BF16)
    total = None
    for i in range(4):
        term = dot_t(held[:, level_lanes(i)], basis_ref[2 + i])
        total = term if total is None else total + term
    out_ref[...] = total


def far_of_halves(core, own_ref, other_ref, levels, basis_ref, held, total):
    for i in range(len(levels)):
        for ref, side in ((own_ref, core), (other_ref, 1 - core)):
            scaled = (ref[:, level_lanes(i)] * factor(levels[i])).astype(BF16)
            for j in range(4):
                held[owned(j, side), level_lanes(i)] = scaled[j * ROWS : (j + 1) * ROWS]
    for i, level in enumerate(levels):
        total += dot_t(held[:, level_lanes(i)], basis_ref[level])
    return total


def far_second_kernel(core_ref, near_ref, basis_ref, own_ref, other_ref, out_ref, held):
    out_ref[...] = far_of_halves(
        core_ref[0], own_ref, other_ref, (0, 1, 2), basis_ref, held, near_ref[...]
    )


def far_high(core, own_ref, other_ref, basis_ref, held):
    for i in range(2):
        lanes = slice(i * LANES, (i + 1) * LANES)
        half = held.at[:, level_lanes(i)]
        half[:, own_half(core)] = (own_ref[:, lanes] * factor(6 + i)).astype(BF16)
        half[:, own_half(1 - core)] = (other_ref[:, lanes] * factor(6 + i)).astype(BF16)
    return dot_t(held[:, level_lanes(0)], basis_ref[6]) + dot_t(
        held[:, level_lanes(1)], basis_ref[7]
    )


def give_halves(core, full_ref, send_ref, keep_ref):
    for i in range(4):
        to = slice(i * ROWS, (i + 1) * ROWS)
        send_ref[to, :] = full_ref[owned(i, 1 - core), :]
        keep_ref[to, :] = full_ref[owned(i, core), :]


def middle_kernel(core_ref, own_ref, other_ref, *refs):
    basis_ref, base_ref, low_ref, image_ref, far_ref, send_ref, keep_ref, held, full = refs
    core = core_ref[0]
    far = low_ref[...] + far_high(core, own_ref, other_ref, basis_ref, held)
    far_ref[...] = far
    image = base_ref[...] + far
    image_ref[...] = image
    coefficients(image.astype(BF16), basis_ref, range(LEVELS), full)
    give_halves(core, full, send_ref, keep_ref)


def dots_kernel(core_ref, base_ref, far_ref, image_ref, near_ref, v_ref, values_ref, high0, high1, gate_ref, *refs):
    send_ref, keep_ref, block_ref = refs
    far, near, image, v = far_ref[...], near_ref[...], image_ref[...], v_ref[...]
    rounded = far.astype(BF16)
    half = LEAF // 2
    own = (
        dot(rounded[:, :half], high0[...])
        + dot(rounded[:, half:], high1[...])
        + values_ref[3:4, :] * far
    )
    curve = base_ref[...] * near + far * (2.0 * near + own)
    lane = lax.broadcasted_iota(jnp.int32, (PROBES, LANES), 1)
    block = jnp.zeros((PROBES, LANES), F32)
    for i, term in enumerate((v * v, v * image, image * image, curve)):
        block = jnp.where(lane == i, jnp.sum(term, axis=1, keepdims=True), block)
    block_ref[...] = block
    give_halves(core_ref[0], block_ref, send_ref, keep_ref)


def final_kernel(core_ref, own_ref, other_ref, basis_ref, low_ref, image_ref, v_ref, x_ref, r_ref, held, dots):
    core = core_ref[0]
    for ref, side in ((own_ref, core), (other_ref, 1 - core)):
        for j in range(4):
            dots[owned(j, side), :] = ref[j * ROWS : (j + 1) * ROWS, 5 * RANK :]
    second = far_of_halves(
        core, own_ref, other_ref, (3, 4, 5, 6, 7), basis_ref, held, low_ref[...]
    )
    m0, m1, m2, m3 = (dots[:, i : i + 1] for i in range(4))
    alpha = m0 / m1
    ratio = m2 / m1
    norm = alpha * alpha * m2 - m0
    curve = alpha * alpha * (m3 - ratio * m2)
    alpha_next = norm / curve
    grown = alpha * ratio
    v = v_ref[...]
    image = image_ref[...]
    x_ref[...] = alpha * v + alpha_next * (grown * v - alpha * image)
    r_ref[...] = v - alpha * image - alpha_next * (grown * image - alpha * second)


def assemble_kernel(y_ref, b0, b1, b2, b3, out_ref):
    for k, back in enumerate((b0, b1, b2, b3)):
        out_ref[quarter(y_ref[0], k), :] = back[:, 4 * RANK :]


def pair_dot(a, b, level):
    return 2.0 * factor(level) * jnp.sum(a * b, axis=1, keepdims=True)


def in_lane(i, x):
    lane = lax.broadcasted_iota(jnp.int32, (PART, LANES), 1)
    return jnp.where(lane == i, x, 0.0)


def sum_kernel(r0, r1, r2, r3, gate_ref, total_ref):
    total_ref[...] = (r0[...] + r1[...]) + (r2[...] + r3[...])


def shift_kernel(own, other, out_ref):
    out_ref[...] = own[:, RANK:] + other[:, RANK:]


def six_seven_kernel(own, other, *refs):
    six_ref, seven_ref = refs[-2:]
    six, seven = slice(2 * RANK, 2 * RANK + LANES), slice(2 * RANK + LANES, 3 * RANK)
    six_ref[...] = own[:, six] + other[:, six]
    seven_ref[...] = own[:, seven] + other[:, seven]


def join_first_kernel(two, three, four, own, x1, x2, x3, gate_ref, out_ref):
    out_ref[:, level_lanes(0)] = two[:, :RANK]
    out_ref[:, level_lanes(1)] = three[:, :RANK]
    out_ref[:, level_lanes(2)] = four[:, :RANK]
    out_ref[:, level_lanes(3)] = own[:, level_lanes(1)] + four[:, level_lanes(1)]
    out_ref[:, 4 * RANK : 4 * RANK + LANES] = x1[...]
    out_ref[:, 4 * RANK + LANES :] = x2[...] + x3[...]


def merge_kernel(y_ref, keep_ref, other_ref, keep_dots, other_dots, *parts):
    end = 6 * RANK
    for k, part_ref in enumerate(parts):
        at = pl.ds(pl.multiple_of((y_ref[0] ^ k) * ROWS, ROWS), ROWS)
        for level in range(6):
            part_ref[:, level_lanes(2 * level)] = keep_ref[at, level_lanes(level)]
            part_ref[:, level_lanes(2 * level + 1)] = other_ref[at, level_lanes(level)]
        part_ref[:, 2 * end : -LANES] = keep_ref[at, end:] + other_ref[at, end:]
        part_ref[:, -LANES:] = keep_dots[at, :] + other_dots[at, :]


def add_dot(total_ref, lane, term):
    lanes = lax.broadcasted_iota(jnp.int32, (ROWS, LANES), 1)
    total_ref[:, -LANES:] += jnp.where(lanes == lane, term, 0.0)


def y_dots_kernel(r0, r1, r2, r3, gate_ref, total_ref):
    pair = 2 * RANK
    start = 2 * pair
    total_ref[...] = (r0[:, start:] + r1[:, start:]) + (r2[:, start:] + r3[:, start:])
    a, b = slice(0, pair), slice(pair, start)
    term = pair_dot(r0[:, a], r1[:, a], 0) + pair_dot(r2[:, a], r3[:, a], 0)
    term += pair_dot(r0[:, b] + r1[:, b], r2[:, b] + r3[:, b], 1)
    add_dot(total_ref, 3, term)


def step_kernel(level, own, other, *rest):
    total_ref = rest[-1]
    pair = 2 * RANK
    total_ref[...] = own[:, pair:] + other[:, pair:]
    add_dot(total_ref, 3, pair_dot(own[:, :pair], other[:, :pair], level))


def core_dots_kernel(own, total_ref):
    total_ref[...] = own[:, 2 * RANK :]
    add_dot(total_ref, 3, pair_dot(own[:, level_lanes(0)], own[:, level_lanes(1)], 5))


def low_join_kernel(r0, r1, r2, r3, two, gate_ref, *outs):
    r = (r0, r1, r2, r3)
    pair = 2 * RANK
    zero, one = slice(0, pair), slice(pair, 2 * pair)
    for k, out in enumerate(outs):
        out[:, zero] = r[k ^ 1][:, zero]
        out[:, one] = r[k ^ 2][:, one] + r[k ^ 3][:, one]
        out[:, 2 * pair :] = two[:, :pair]


def high_join_kernel(three, four, five, own, x1, x2, x3, out_ref):
    a, b, q = slice(0, RANK), slice(RANK, 2 * RANK), slice(2 * RANK, 2 * RANK + LANES)
    far = x2[:, b] + x3[:, b]
    pair = 2 * RANK
    out_ref[:, :pair] = three[:, :pair]
    out_ref[:, pair : 2 * pair] = four[:, :pair]
    out_ref[:, level_lanes(4)] = five[:, level_lanes(1)]
    out_ref[:, level_lanes(5)] = five[:, level_lanes(0)]
    out_ref[:, level_lanes(6)] = x1[:, a]
    out_ref[:, level_lanes(7)] = far
    out_ref[:, 8 * RANK :] = (own[:, q] + x1[:, q]) + (x2[:, q] + x3[:, q])
    term = pair_dot(own[:, a], x1[:, a], 6) + pair_dot(x2[:, a], x3[:, a], 6)
    term += pair_dot(own[:, b] + x1[:, b], far, 7)
    add_dot(out_ref, 3, term)


def gather_kernel_of(levels, shared, y_ref, b0, b1, b2, b3, *rest):
    own_ref, send_ref = rest[-2:]
    for k, back in enumerate((b0, b1, b2, b3)):
        at = pl.ds(pl.multiple_of((y_ref[0] ^ k) * ROWS, ROWS), ROWS)
        for i in range(levels):
            own_ref[at, level_lanes(i)] = back[:, level_lanes(2 * i)]
            send_ref[at, level_lanes(i)] = back[:, level_lanes(2 * i + 1)]
        if shared:
            own_ref[at, levels * RANK :] = back[:, 2 * levels * RANK :]
            send_ref[at, levels * RANK :] = back[:, 2 * levels * RANK :]


def swap(x, axis, mask):
    return lax.ppermute(x, axis, [(i, i ^ mask) for i in range(lax.axis_size(axis))])


def over_y(x):
    return [x[0]] + [swap(x[k], "local", k) for k in (1, 2, 3)]


Z1, Z2, Z3 = ("local", 4), ("local", 8), ("local", 24)
CORE, X1, X2, X3 = ("group", 1), ("group", 2), ("group", 4), ("group", 6)


def rows(lanes):
    return shape(ROWS, lanes)


def part(lanes):
    return shape(PART, lanes)


def per_device(coords, inv_length, noise, order, basis, probes):
    y = (lax.axis_index("local") & 3).astype(jnp.int32)[None]
    core = (lax.axis_index("group") & 1).astype(jnp.int32)[None]
    flat = basis.reshape(LEAF * LEVELS, RANK)
    square = shape(LEAF // 2, LEAF, dtype=BF16)
    vectors = shape(PROBES, LEAF)
    both = shape(PROBES, RANK)

    basis, send, keep, low = call(
        start_kernel,
        (
            shape(LEVELS, LEAF, RANK, dtype=BF16),
            shape(PROBES, 2 * RANK),
            both,
            shape(PROBES, 3 * RANK),
        ),
        core,
        pltpu.with_memory_space_constraint(probes, pltpu.HBM),
        pltpu.with_memory_space_constraint(flat, pltpu.HBM),
        scratch=[
            pltpu.VMEM((PROBES, 2 * RANK), F32),
            pltpu.VMEM((LEAF * LEVELS, RANK), BF16),
            pltpu.VMEM((LEVELS, LEAF, RANK), BF16),
            pltpu.VMEM((PROBES, LEAF), F32),
            pltpu.SemaphoreType.DMA((2 * CHUNKS + 1,)),
        ],
        smem=1,
        outside=2,
        flops=2**31,
        limit=START_LIMIT,
        outs=(ANY, VMEM, VMEM, VMEM),
    )
    other = swap(send, *CORE)
    parts = call(parts_kernel, (part(5 * RANK),) * 4, y, low, keep, other, smem=1)
    moved = over_y(parts)

    values = jnp.concatenate(
        [coords * inv_length[:, None], noise[None, :], jnp.zeros((4, LEAF), F32)], axis=0
    )
    values = call(
        gather_kernel, shape(8, LEAF), order, values, parts[0], anywhere=1, flops=2**26
    )
    high0, low0 = call(
        functools.partial(matrix_kernel, 0), (square, square), values, flops=2**30
    )
    high1, low1 = call(
        functools.partial(matrix_kernel, 1), (square, square), values, flops=2**30
    )
    matrix = (values, high0, high1, low0, low1)
    near = call(near_kernel, vectors, probes, *matrix, flops=2**30)

    total = call(sum_kernel, part(5 * RANK), *moved, near, anywhere=1)
    two = swap(total, *Z1)
    leaf = call(
        functools.partial(whole_kernel, (0, 1)),
        shape(PROBES, 2 * RANK),
        probes,
        basis,
        total,
        anywhere=1,
        flops=2**28,
    )
    leaf_other = swap(leaf, "local", 1)
    total = call(shift_kernel, part(4 * RANK), total, two)
    three = swap(total, *Z2)
    leaf_next = call(shift_kernel, both, leaf, leaf_other)
    one = swap(leaf_next, "local", 3)
    total = call(shift_kernel, part(3 * RANK), total, three)
    four = swap(total, *Z3)
    six, seven = call(
        six_seven_kernel, (part(LANES),) * 2, total, four, one, anywhere=1
    )
    x1, x2, x3 = swap(six, *X1), swap(seven, *X2), swap(seven, *X3)
    base = call(base_kernel, vectors, near, basis, leaf_other, one, flops=2**28)
    base_near = call(near_kernel, vectors, base, *matrix, flops=2**30)
    back = call(
        join_first_kernel,
        part(5 * RANK),
        two,
        three,
        four,
        total,
        x1,
        x2,
        x3,
        base_near,
        anywhere=1,
    )
    back = over_y([back] * 4)
    own = call(assemble_kernel, both, y, *back, smem=1)
    other = swap(own, *CORE)
    far = call(
        far_first_kernel,
        vectors,
        y,
        basis,
        *back,
        scratch=[pltpu.VMEM((PROBES, 4 * RANK), BF16)],
        smem=1,
        flops=2**29,
    )
    wide, half = LEVELS * RANK, PROBES // 2
    image, far, send, keep = call(
        middle_kernel,
        (vectors, vectors, shape(half, wide), shape(half, wide)),
        core,
        own,
        other,
        basis,
        base,
        far,
        scratch=[pltpu.VMEM((PROBES, 2 * RANK), BF16), pltpu.VMEM((PROBES, wide), F32)],
        smem=1,
        flops=2**30,
    )
    other = swap(send, *CORE)
    send, keep_dots = call(
        dots_kernel,
        (shape(half, LANES), shape(half, LANES)),
        core,
        base,
        far,
        image,
        base_near,
        probes,
        values,
        high0,
        high1,
        send,
        scratch=[pltpu.VMEM((PROBES, LANES), F32)],
        smem=1,
        anywhere=1,
        flops=2**28,
    )
    other_dots = swap(send, *CORE)
    parts = call(
        merge_kernel,
        (rows(14 * RANK + LANES),) * 4,
        y,
        keep,
        other,
        keep_dots,
        other_dots,
        smem=1,
    )
    moved = over_y(parts)
    near = call(
        near_kernel, vectors, image, *matrix, parts[0], anywhere=1, flops=2**30
    )
    total = call(
        y_dots_kernel, rows(10 * RANK + LANES), *moved, near, anywhere=1
    )
    two = swap(total, *Z1)
    total = call(functools.partial(step_kernel, 2), rows(8 * RANK + LANES), total, two)
    three = swap(total, *Z2)
    back = call(low_join_kernel, (rows(6 * RANK),) * 4, *moved, two, total, anywhere=1)
    back = over_y(back)
    total = call(functools.partial(step_kernel, 3), rows(6 * RANK + LANES), total, three)
    four = swap(total, *Z3)
    five = call(
        functools.partial(step_kernel, 4),
        rows(4 * RANK + LANES),
        total,
        four,
        *back[1:],
        anywhere=3,
    )
    total = call(core_dots_kernel, rows(2 * RANK + LANES), five)
    x1, x2, x3 = swap(total, *X1), swap(total, *X2), swap(total, *X3)
    low_own, send = call(
        functools.partial(gather_kernel_of, 3, False),
        (shape(PROBES // 2, 3 * RANK),) * 2,
        y,
        *back,
        smem=1,
    )
    low_other = swap(send, *CORE)
    high_back = call(
        high_join_kernel, rows(8 * RANK + LANES), three, four, five, total, x1, x2, x3
    )
    high_back = over_y([high_back] * 4)
    partial_second = call(
        far_second_kernel,
        vectors,
        core,
        near,
        basis,
        low_own,
        low_other,
        scratch=[pltpu.VMEM((PROBES, 3 * RANK), BF16)],
        smem=1,
        flops=2**29,
    )
    own, send = call(
        functools.partial(gather_kernel_of, 3, True),
        (shape(PROBES // 2, 5 * RANK + LANES),) * 2,
        y,
        *high_back,
        partial_second,
        smem=1,
        anywhere=1,
    )
    other = swap(send, *CORE)
    return call(
        final_kernel,
        (vectors, vectors),
        core,
        own,
        other,
        basis,
        partial_second,
        image,
        probes,
        scratch=[pltpu.VMEM((PROBES, 5 * RANK), BF16), pltpu.VMEM((PROBES, LANES), F32)],
        smem=1,
        flops=2**29,
    )


def solution(mesh):
    in_specs = (
        P(None, ("group", "local")),
        P(),
        P(("group", "local")),
        P(("group", "local"), None),
        P(("group", "local"), None, None),
        P(None, ("group", "local")),
    )
    out_specs = (P(None, ("group", "local")), P(None, ("group", "local")))
    return jax.shard_map(
        per_device, mesh=mesh, in_specs=in_specs, out_specs=out_specs, check_vma=False
    )
```

```python
import functools
import math

import jax
import jax.numpy as jnp
from jax import lax
from jax.experimental import pallas as pl
from jax.experimental.pallas import tpu as pltpu
from jax.sharding import PartitionSpec as P

GAMMA = 0.08
ROOT_OF_THREE = math.sqrt(3.0)
SHIFT = 3.5
LEVELS = 8
RANK = 256
LEAF = 1024
PROBES = 128
PART = PROBES // 4
ROWS = PART // 2
LANES = 128
CHUNKS = 8
START_LIMIT = 52
F32 = jnp.float32
BF16 = jnp.bfloat16
VMEM = pl.BlockSpec(memory_space=pltpu.VMEM)
SMEM = pl.BlockSpec(memory_space=pltpu.SMEM)
ANY = pl.BlockSpec(memory_space=pl.ANY)
HBM = pl.BlockSpec(memory_space=pltpu.HBM)


def factor(level):
    return GAMMA / (LEAF * 2.0**level)


def call(kernel, out_shape, *args, scratch=(), smem=0, anywhere=0, outside=0, flops=0, limit=16, outs=None):
    held = len(args) - smem - anywhere - outside
    return pl.pallas_call(
        kernel,
        out_shape=out_shape,
        in_specs=[SMEM] * smem + [VMEM] * held + [ANY] * anywhere + [HBM] * outside,
        out_specs=outs or jax.tree.map(lambda _: VMEM, out_shape),
        scratch_shapes=list(scratch),
        compiler_params=pltpu.CompilerParams(vmem_limit_bytes=limit * 2**20),
        cost_estimate=pl.CostEstimate(
            flops=flops, bytes_accessed=2**20, transcendentals=0
        ),
    )(*args)


def shape(*dims, dtype=F32):
    return jax.ShapeDtypeStruct(dims, dtype)


def dot(a, b):
    return jnp.dot(a, b, preferred_element_type=F32)


def dot_t(a, b):
    return lax.dot_general(a, b, (((1,), (1,)), ((), ())), preferred_element_type=F32)


def split(x):
    high = x.astype(BF16)
    return high, (x - high.astype(F32)).astype(BF16)


def level_lanes(i):
    return slice(i * RANK, (i + 1) * RANK)


def owned(i, core):
    return pl.ds(pl.multiple_of(i * PART + core * ROWS, ROWS), ROWS)


def quarter(y, k):
    return pl.ds(pl.multiple_of((y ^ k) * PART, PART), PART)


def coefficients(v, basis_ref, levels, full_ref):
    for i, level in enumerate(levels):
        full_ref[:, level_lanes(i)] = dot(v, basis_ref[level])


def own_half(core):
    return pl.ds(pl.multiple_of(core * LANES, LANES), LANES)


def scatter_halves(core, full_ref, send_ref, keep_ref, at):
    for i in range(2):
        lanes = slice(i * LANES, (i + 1) * LANES)
        half = full_ref.at[:, level_lanes(i)]
        keep_ref[:, lanes] = half[:, own_half(core)]
        send_ref[:, at + i * LANES : at + (i + 1) * LANES] = half[:, own_half(1 - core)]


def start_kernel(core_ref, v_hbm, flat_ref, basis_out, send_ref, keep_ref, low_ref, full, held, basis_ref, v_ref, sems):
    rows = LEAF * LEVELS // CHUNKS
    points = LEAF // CHUNKS
    copies = [
        pltpu.make_async_copy(
            flat_ref.at[pl.ds(i * rows, rows)], held.at[pl.ds(i * rows, rows)], sems.at[i]
        )
        for i in range(CHUNKS)
    ]
    saves = [
        pltpu.make_async_copy(
            basis_ref.at[:, pl.ds(i * points, points)],
            basis_out.at[:, pl.ds(i * points, points)],
            sems.at[CHUNKS + 1 + i],
        )
        for i in range(CHUNKS)
    ]
    last = pltpu.make_async_copy(v_hbm, v_ref, sems.at[CHUNKS])
    for copy in copies:
        copy.start()
    last.start()
    width = 32
    block = width * LEVELS
    to = lax.broadcasted_iota(jnp.int32, (block, block), 0)
    at = lax.broadcasted_iota(jnp.int32, (block, block), 1)
    source = (to & (width - 1)) * LEVELS + (to >> 5)
    order = jnp.where(at == source, 1.0, 0.0).astype(BF16)
    for i, copy in enumerate(copies):
        copy.wait()
        for j in range(i * rows // block, (i + 1) * rows // block):
            moved = dot(order, held[j * block : (j + 1) * block, :]).astype(BF16)
            for level in range(LEVELS):
                basis_ref[level, j * width : (j + 1) * width, :] = moved[
                    level * width : (level + 1) * width
                ]
        saves[i].start()
    last.wait()
    v = v_ref[...].astype(BF16)
    send_ref[:, :RANK] = dot(v, basis_ref[5])
    coefficients(v, basis_ref, (6, 7), full)
    scatter_halves(core_ref[0], full, send_ref, keep_ref, RANK)
    coefficients(v, basis_ref, (2, 3, 4), low_ref)
    for save in saves:
        save.wait()


def whole_kernel(levels, v_ref, basis_ref, gate_ref, out_ref):
    coefficients(v_ref[...].astype(BF16), basis_ref, levels, out_ref)


def parts_kernel(y_ref, low_ref, keep_ref, other_ref, *parts):
    for k, part in enumerate(parts):
        at = quarter(y_ref[0], k)
        part[:, : 3 * RANK] = low_ref[at, :]
        part[:, 3 * RANK : 4 * RANK] = other_ref[at, :RANK]
        part[:, 4 * RANK :] = keep_ref[at, :] + other_ref[at, RANK:]


def gather_kernel(order_ref, values_ref, gate_ref, out_ref):
    x = values_ref[...]
    a, rest = x.astype(BF16), x - x.astype(BF16).astype(F32)
    b, c = split(rest)
    pieces = jnp.concatenate([a, b, c], axis=0)
    step = 256
    total = None
    for i in range(LEAF // step):
        source = lax.broadcasted_iota(jnp.int32, (step, LEAF), 0) + i * step
        hot = jnp.where(source == order_ref[...], 1.0, 0.0).astype(BF16)
        term = dot(pieces[:, i * step : (i + 1) * step], hot)
        total = term if total is None else total + term
    out_ref[...] = total[:8] + total[8:16] + total[16:]


def matrix_kernel(half, values_ref, high_ref, low_ref):
    step = 128
    columns = values_ref[...].T
    for i in range(LEAF // 2 // step):
        at = slice(half * LEAF // 2 + i * step, half * LEAF // 2 + (i + 1) * step)
        square = None
        for c in range(3):
            diff = columns[at, c : c + 1] - values_ref[c : c + 1, :]
            square = diff * diff if square is None else square + diff * diff
        t = ROOT_OF_THREE * jnp.sqrt(square)
        high, low = split((1.0 + t) * jnp.exp(-t))
        high_ref[i * step : (i + 1) * step, :] = high
        low_ref[i * step : (i + 1) * step, :] = low


def near_kernel(v_ref, values_ref, high0, high1, low0, low1, *rest):
    out_ref = rest[-1]
    v = v_ref[...]
    v_high, v_low = split(v)
    both = LEAF // 2
    first, second = slice(0, both), slice(both, LEAF)
    out_ref[...] = (
        (dot(v_low[:, first], high0[...]) + dot(v_low[:, second], high1[...]))
        + (dot(v_high[:, first], low0[...]) + dot(v_high[:, second], low1[...]))
        + (dot(v_high[:, first], high0[...]) + dot(v_high[:, second], high1[...]))
        + values_ref[3:4, :] * v
    )


def base_kernel(near_ref, v_ref, basis_ref, sib0, sib1, out_ref):
    zero = (sib0[:, :RANK] * factor(0)).astype(BF16)
    one = (sib1[...] * factor(1)).astype(BF16)
    out_ref[...] = (
        (near_ref[...] - SHIFT * v_ref[...])
        + dot_t(zero, basis_ref[0])
        + dot_t(one, basis_ref[1])
    )


def far_first_kernel(y_ref, basis_ref, b0, b1, b2, b3, out_ref, held):
    for k, back in enumerate((b0, b1, b2, b3)):
        for i in range(4):
            held[quarter(y_ref[0], k), level_lanes(i)] = (
                back[:, level_lanes(i)] * factor(2 + i)
            ).astype(BF16)
    total = None
    for i in range(4):
        term = dot_t(held[:, level_lanes(i)], basis_ref[2 + i])
        total = term if total is None else total + term
    out_ref[...] = total


def far_of_halves(core, own_ref, other_ref, levels, basis_ref, held, total):
    for i in range(len(levels)):
        for ref, side in ((own_ref, core), (other_ref, 1 - core)):
            scaled = (ref[:, level_lanes(i)] * factor(levels[i])).astype(BF16)
            for j in range(4):
                held[owned(j, side), level_lanes(i)] = scaled[j * ROWS : (j + 1) * ROWS]
    for i, level in enumerate(levels):
        total += dot_t(held[:, level_lanes(i)], basis_ref[level])
    return total


def far_second_kernel(core_ref, near_ref, basis_ref, own_ref, other_ref, out_ref, held):
    out_ref[...] = far_of_halves(
        core_ref[0], own_ref, other_ref, (0, 1, 2), basis_ref, held, near_ref[...]
    )


def far_high(core, own_ref, other_ref, basis_ref, held):
    for i in range(2):
        lanes = slice(i * LANES, (i + 1) * LANES)
        half = held.at[:, level_lanes(i)]
        half[:, own_half(core)] = (own_ref[:, lanes] * factor(6 + i)).astype(BF16)
        half[:, own_half(1 - core)] = (other_ref[:, lanes] * factor(6 + i)).astype(BF16)
    return dot_t(held[:, level_lanes(0)], basis_ref[6]) + dot_t(
        held[:, level_lanes(1)], basis_ref[7]
    )


def give_halves(core, full_ref, send_ref, keep_ref):
    for i in range(4):
        to = slice(i * ROWS, (i + 1) * ROWS)
        send_ref[to, :] = full_ref[owned(i, 1 - core), :]
        keep_ref[to, :] = full_ref[owned(i, core), :]


def middle_kernel(core_ref, own_ref, other_ref, *refs):
    basis_ref, base_ref, low_ref, image_ref, far_ref, send_ref, keep_ref, held, full = refs
    core = core_ref[0]
    far = low_ref[...] + far_high(core, own_ref, other_ref, basis_ref, held)
    far_ref[...] = far
    image = base_ref[...] + far
    image_ref[...] = image
    coefficients(image.astype(BF16), basis_ref, range(LEVELS), full)
    give_halves(core, full, send_ref, keep_ref)


def dots_kernel(core_ref, base_ref, far_ref, image_ref, near_ref, v_ref, values_ref, high0, high1, gate_ref, *refs):
    send_ref, keep_ref, block_ref = refs
    far, near, image, v = far_ref[...], near_ref[...], image_ref[...], v_ref[...]
    rounded = far.astype(BF16)
    half = LEAF // 2
    own = (
        dot(rounded[:, :half], high0[...])
        + dot(rounded[:, half:], high1[...])
        + values_ref[3:4, :] * far
    )
    curve = base_ref[...] * near + far * (2.0 * near + own)
    lane = lax.broadcasted_iota(jnp.int32, (PROBES, LANES), 1)
    block = jnp.zeros((PROBES, LANES), F32)
    for i, term in enumerate((v * v, v * image, image * image, curve)):
        block = jnp.where(lane == i, jnp.sum(term, axis=1, keepdims=True), block)
    block_ref[...] = block
    give_halves(core_ref[0], block_ref, send_ref, keep_ref)


def final_kernel(core_ref, own_ref, other_ref, basis_ref, low_ref, image_ref, v_ref, x_ref, r_ref, held, dots):
    core = core_ref[0]
    for ref, side in ((own_ref, core), (other_ref, 1 - core)):
        for j in range(4):
            dots[owned(j, side), :] = ref[j * ROWS : (j + 1) * ROWS, 5 * RANK :]
    second = far_of_halves(
        core, own_ref, other_ref, (3, 4, 5, 6, 7), basis_ref, held, low_ref[...]
    )
    n0, n1, n2, n3 = (dots[:, i : i + 1] for i in range(4))
    m1 = n1 + SHIFT * n0
    mixed = n2 + SHIFT * n1
    alpha = n0 / m1
    norm = alpha * (alpha * n2 - n1 * (n1 / m1))
    curve = alpha * alpha * (n3 - mixed * (mixed / m1))
    alpha_next = norm / curve
    grown = alpha * (mixed / m1)
    v = v_ref[...]
    shifted = image_ref[...]
    image = shifted + SHIFT * v
    x_ref[...] = alpha * v + alpha_next * (grown * v - alpha * shifted)
    r_ref[...] = (n1 / m1) * v - alpha * shifted - alpha_next * (grown * image - alpha * second)


def assemble_kernel(y_ref, b0, b1, b2, b3, out_ref):
    for k, back in enumerate((b0, b1, b2, b3)):
        out_ref[quarter(y_ref[0], k), :] = back[:, 4 * RANK :]


def pair_dot(a, b, level):
    return 2.0 * factor(level) * jnp.sum(a * b, axis=1, keepdims=True)


def in_lane(i, x):
    lane = lax.broadcasted_iota(jnp.int32, (PART, LANES), 1)
    return jnp.where(lane == i, x, 0.0)


def sum_kernel(r0, r1, r2, r3, gate_ref, total_ref):
    total_ref[...] = (r0[...] + r1[...]) + (r2[...] + r3[...])


def shift_kernel(own, other, out_ref):
    out_ref[...] = own[:, RANK:] + other[:, RANK:]


def six_seven_kernel(own, other, *refs):
    six_ref, seven_ref = refs[-2:]
    six, seven = slice(2 * RANK, 2 * RANK + LANES), slice(2 * RANK + LANES, 3 * RANK)
    six_ref[...] = own[:, six] + other[:, six]
    seven_ref[...] = own[:, seven] + other[:, seven]


def join_first_kernel(two, three, four, own, x1, x2, x3, gate_ref, out_ref):
    out_ref[:, level_lanes(0)] = two[:, :RANK]
    out_ref[:, level_lanes(1)] = three[:, :RANK]
    out_ref[:, level_lanes(2)] = four[:, :RANK]
    out_ref[:, level_lanes(3)] = own[:, level_lanes(1)] + four[:, level_lanes(1)]
    out_ref[:, 4 * RANK : 4 * RANK + LANES] = x1[...]
    out_ref[:, 4 * RANK + LANES :] = x2[...] + x3[...]


def merge_kernel(y_ref, keep_ref, other_ref, keep_dots, other_dots, *parts):
    end = 6 * RANK
    for k, part_ref in enumerate(parts):
        at = pl.ds(pl.multiple_of((y_ref[0] ^ k) * ROWS, ROWS), ROWS)
        for level in range(6):
            part_ref[:, level_lanes(2 * level)] = keep_ref[at, level_lanes(level)]
            part_ref[:, level_lanes(2 * level + 1)] = other_ref[at, level_lanes(level)]
        part_ref[:, 2 * end : -LANES] = keep_ref[at, end:] + other_ref[at, end:]
        part_ref[:, -LANES:] = keep_dots[at, :] + other_dots[at, :]


def add_dot(total_ref, lane, term):
    lanes = lax.broadcasted_iota(jnp.int32, (ROWS, LANES), 1)
    total_ref[:, -LANES:] += jnp.where(lanes == lane, term, 0.0)


def y_dots_kernel(r0, r1, r2, r3, gate_ref, total_ref):
    pair = 2 * RANK
    start = 2 * pair
    total_ref[...] = (r0[:, start:] + r1[:, start:]) + (r2[:, start:] + r3[:, start:])
    a, b = slice(0, pair), slice(pair, start)
    term = pair_dot(r0[:, a], r1[:, a], 0) + pair_dot(r2[:, a], r3[:, a], 0)
    term += pair_dot(r0[:, b] + r1[:, b], r2[:, b] + r3[:, b], 1)
    add_dot(total_ref, 3, term)


def step_kernel(level, own, other, *rest):
    total_ref = rest[-1]
    pair = 2 * RANK
    total_ref[...] = own[:, pair:] + other[:, pair:]
    add_dot(total_ref, 3, pair_dot(own[:, :pair], other[:, :pair], level))


def core_dots_kernel(own, total_ref):
    total_ref[...] = own[:, 2 * RANK :]
    add_dot(total_ref, 3, pair_dot(own[:, level_lanes(0)], own[:, level_lanes(1)], 5))


def low_join_kernel(r0, r1, r2, r3, two, gate_ref, *outs):
    r = (r0, r1, r2, r3)
    pair = 2 * RANK
    zero, one = slice(0, pair), slice(pair, 2 * pair)
    for k, out in enumerate(outs):
        out[:, zero] = r[k ^ 1][:, zero]
        out[:, one] = r[k ^ 2][:, one] + r[k ^ 3][:, one]
        out[:, 2 * pair :] = two[:, :pair]


def high_join_kernel(three, four, five, own, x1, x2, x3, out_ref):
    a, b, q = slice(0, RANK), slice(RANK, 2 * RANK), slice(2 * RANK, 2 * RANK + LANES)
    far = x2[:, b] + x3[:, b]
    pair = 2 * RANK
    out_ref[:, :pair] = three[:, :pair]
    out_ref[:, pair : 2 * pair] = four[:, :pair]
    out_ref[:, level_lanes(4)] = five[:, level_lanes(1)]
    out_ref[:, level_lanes(5)] = five[:, level_lanes(0)]
    out_ref[:, level_lanes(6)] = x1[:, a]
    out_ref[:, level_lanes(7)] = far
    out_ref[:, 8 * RANK :] = (own[:, q] + x1[:, q]) + (x2[:, q] + x3[:, q])
    term = pair_dot(own[:, a], x1[:, a], 6) + pair_dot(x2[:, a], x3[:, a], 6)
    term += pair_dot(own[:, b] + x1[:, b], far, 7)
    add_dot(out_ref, 3, term)


def gather_kernel_of(levels, shared, y_ref, b0, b1, b2, b3, *rest):
    own_ref, send_ref = rest[-2:]
    for k, back in enumerate((b0, b1, b2, b3)):
        at = pl.ds(pl.multiple_of((y_ref[0] ^ k) * ROWS, ROWS), ROWS)
        for i in range(levels):
            own_ref[at, level_lanes(i)] = back[:, level_lanes(2 * i)]
            send_ref[at, level_lanes(i)] = back[:, level_lanes(2 * i + 1)]
        if shared:
            own_ref[at, levels * RANK :] = back[:, 2 * levels * RANK :]
            send_ref[at, levels * RANK :] = back[:, 2 * levels * RANK :]


def swap(x, axis, mask):
    return lax.ppermute(x, axis, [(i, i ^ mask) for i in range(lax.axis_size(axis))])


def over_y(x):
    return [x[0]] + [swap(x[k], "local", k) for k in (1, 2, 3)]


Z1, Z2, Z3 = ("local", 4), ("local", 8), ("local", 24)
CORE, X1, X2, X3 = ("group", 1), ("group", 2), ("group", 4), ("group", 6)


def rows(lanes):
    return shape(ROWS, lanes)


def part(lanes):
    return shape(PART, lanes)


def per_device(coords, inv_length, noise, order, basis, probes):
    y = (lax.axis_index("local") & 3).astype(jnp.int32)[None]
    core = (lax.axis_index("group") & 1).astype(jnp.int32)[None]
    flat = basis.reshape(LEAF * LEVELS, RANK)
    square = shape(LEAF // 2, LEAF, dtype=BF16)
    vectors = shape(PROBES, LEAF)
    both = shape(PROBES, RANK)

    basis, send, keep, low = call(
        start_kernel,
        (
            shape(LEVELS, LEAF, RANK, dtype=BF16),
            shape(PROBES, 2 * RANK),
            both,
            shape(PROBES, 3 * RANK),
        ),
        core,
        pltpu.with_memory_space_constraint(probes, pltpu.HBM),
        pltpu.with_memory_space_constraint(flat, pltpu.HBM),
        scratch=[
            pltpu.VMEM((PROBES, 2 * RANK), F32),
            pltpu.VMEM((LEAF * LEVELS, RANK), BF16),
            pltpu.VMEM((LEVELS, LEAF, RANK), BF16),
            pltpu.VMEM((PROBES, LEAF), F32),
            pltpu.SemaphoreType.DMA((2 * CHUNKS + 1,)),
        ],
        smem=1,
        outside=2,
        flops=2**31,
        limit=START_LIMIT,
        outs=(ANY, VMEM, VMEM, VMEM),
    )
    other = swap(send, *CORE)
    parts = call(parts_kernel, (part(5 * RANK),) * 4, y, low, keep, other, smem=1)
    moved = over_y(parts)

    values = jnp.concatenate(
        [coords * inv_length[:, None], noise[None, :], jnp.zeros((4, LEAF), F32)], axis=0
    )
    values = call(
        gather_kernel, shape(8, LEAF), order, values, parts[0], anywhere=1, flops=2**26
    )
    high0, low0 = call(
        functools.partial(matrix_kernel, 0), (square, square), values, flops=2**30
    )
    high1, low1 = call(
        functools.partial(matrix_kernel, 1), (square, square), values, flops=2**30
    )
    matrix = (values, high0, high1, low0, low1)
    near = call(near_kernel, vectors, probes, *matrix, flops=2**30)

    total = call(sum_kernel, part(5 * RANK), *moved, near, anywhere=1)
    two = swap(total, *Z1)
    leaf = call(
        functools.partial(whole_kernel, (0, 1)),
        shape(PROBES, 2 * RANK),
        probes,
        basis,
        total,
        anywhere=1,
        flops=2**28,
    )
    leaf_other = swap(leaf, "local", 1)
    total = call(shift_kernel, part(4 * RANK), total, two)
    three = swap(total, *Z2)
    leaf_next = call(shift_kernel, both, leaf, leaf_other)
    one = swap(leaf_next, "local", 3)
    total = call(shift_kernel, part(3 * RANK), total, three)
    four = swap(total, *Z3)
    six, seven = call(
        six_seven_kernel, (part(LANES),) * 2, total, four, one, anywhere=1
    )
    x1, x2, x3 = swap(six, *X1), swap(seven, *X2), swap(seven, *X3)
    base = call(
        base_kernel, vectors, near, probes, basis, leaf_other, one, flops=2**28
    )
    base_near = call(near_kernel, vectors, base, *matrix, flops=2**30)
    back = call(
        join_first_kernel,
        part(5 * RANK),
        two,
        three,
        four,
        total,
        x1,
        x2,
        x3,
        base_near,
        anywhere=1,
    )
    back = over_y([back] * 4)
    own = call(assemble_kernel, both, y, *back, smem=1)
    other = swap(own, *CORE)
    far = call(
        far_first_kernel,
        vectors,
        y,
        basis,
        *back,
        scratch=[pltpu.VMEM((PROBES, 4 * RANK), BF16)],
        smem=1,
        flops=2**29,
    )
    wide, half = LEVELS * RANK, PROBES // 2
    image, far, send, keep = call(
        middle_kernel,
        (vectors, vectors, shape(half, wide), shape(half, wide)),
        core,
        own,
        other,
        basis,
        base,
        far,
        scratch=[pltpu.VMEM((PROBES, 2 * RANK), BF16), pltpu.VMEM((PROBES, wide), F32)],
        smem=1,
        flops=2**30,
    )
    other = swap(send, *CORE)
    send, keep_dots = call(
        dots_kernel,
        (shape(half, LANES), shape(half, LANES)),
        core,
        base,
        far,
        image,
        base_near,
        probes,
        values,
        high0,
        high1,
        send,
        scratch=[pltpu.VMEM((PROBES, LANES), F32)],
        smem=1,
        anywhere=1,
        flops=2**28,
    )
    other_dots = swap(send, *CORE)
    parts = call(
        merge_kernel,
        (rows(14 * RANK + LANES),) * 4,
        y,
        keep,
        other,
        keep_dots,
        other_dots,
        smem=1,
    )
    moved = over_y(parts)
    near = call(
        near_kernel, vectors, image, *matrix, parts[0], anywhere=1, flops=2**30
    )
    total = call(
        y_dots_kernel, rows(10 * RANK + LANES), *moved, near, anywhere=1
    )
    two = swap(total, *Z1)
    total = call(functools.partial(step_kernel, 2), rows(8 * RANK + LANES), total, two)
    three = swap(total, *Z2)
    back = call(low_join_kernel, (rows(6 * RANK),) * 4, *moved, two, total, anywhere=1)
    back = over_y(back)
    total = call(functools.partial(step_kernel, 3), rows(6 * RANK + LANES), total, three)
    four = swap(total, *Z3)
    five = call(
        functools.partial(step_kernel, 4),
        rows(4 * RANK + LANES),
        total,
        four,
        *back[1:],
        anywhere=3,
    )
    total = call(core_dots_kernel, rows(2 * RANK + LANES), five)
    x1, x2, x3 = swap(total, *X1), swap(total, *X2), swap(total, *X3)
    low_own, send = call(
        functools.partial(gather_kernel_of, 3, False),
        (shape(PROBES // 2, 3 * RANK),) * 2,
        y,
        *back,
        smem=1,
    )
    low_other = swap(send, *CORE)
    high_back = call(
        high_join_kernel, rows(8 * RANK + LANES), three, four, five, total, x1, x2, x3
    )
    high_back = over_y([high_back] * 4)
    partial_second = call(
        far_second_kernel,
        vectors,
        core,
        near,
        basis,
        low_own,
        low_other,
        scratch=[pltpu.VMEM((PROBES, 3 * RANK), BF16)],
        smem=1,
        flops=2**29,
    )
    own, send = call(
        functools.partial(gather_kernel_of, 3, True),
        (shape(PROBES // 2, 5 * RANK + LANES),) * 2,
        y,
        *high_back,
        partial_second,
        smem=1,
        anywhere=1,
    )
    other = swap(send, *CORE)
    return call(
        final_kernel,
        (vectors, vectors),
        core,
        own,
        other,
        basis,
        partial_second,
        image,
        probes,
        scratch=[pltpu.VMEM((PROBES, 5 * RANK), BF16), pltpu.VMEM((PROBES, LANES), F32)],
        smem=1,
        flops=2**29,
    )


def solution(mesh):
    in_specs = (
        P(None, ("group", "local")),
        P(),
        P(("group", "local")),
        P(("group", "local"), None),
        P(("group", "local"), None, None),
        P(None, ("group", "local")),
    )
    out_specs = (P(None, ("group", "local")), P(None, ("group", "local")))
    return jax.shard_map(
        per_device, mesh=mesh, in_specs=in_specs, out_specs=out_specs, check_vma=False
    )
```

```python
import functools
import math

import jax
import jax.numpy as jnp
from jax import lax
from jax.experimental import pallas as pl
from jax.experimental.pallas import tpu as pltpu
from jax.sharding import PartitionSpec as P

GAMMA = 0.08
ROOT_OF_THREE = math.sqrt(3.0)
SHIFT = 3.5
LEVELS = 8
RANK = 256
LEAF = 1024
PROBES = 128
PART = PROBES // 4
ROWS = PART // 2
LANES = 128
CHUNKS = 4
START_LIMIT = 52
F32 = jnp.float32
BF16 = jnp.bfloat16
VMEM = pl.BlockSpec(memory_space=pltpu.VMEM)
SMEM = pl.BlockSpec(memory_space=pltpu.SMEM)
ANY = pl.BlockSpec(memory_space=pl.ANY)
HBM = pl.BlockSpec(memory_space=pltpu.HBM)


def factor(level):
    return GAMMA / (LEAF * 2.0**level)


def call(kernel, out_shape, *args, scratch=(), smem=0, anywhere=0, outside=0, flops=0, limit=16, outs=None):
    held = len(args) - smem - anywhere - outside
    return pl.pallas_call(
        kernel,
        out_shape=out_shape,
        in_specs=[SMEM] * smem + [VMEM] * held + [ANY] * anywhere + [HBM] * outside,
        out_specs=outs or jax.tree.map(lambda _: VMEM, out_shape),
        scratch_shapes=list(scratch),
        compiler_params=pltpu.CompilerParams(vmem_limit_bytes=limit * 2**20),
        cost_estimate=pl.CostEstimate(
            flops=flops, bytes_accessed=2**20, transcendentals=0
        ),
    )(*args)


def shape(*dims, dtype=F32):
    return jax.ShapeDtypeStruct(dims, dtype)


def dot(a, b):
    return jnp.dot(a, b, preferred_element_type=F32)


def dot_t(a, b):
    return lax.dot_general(a, b, (((1,), (1,)), ((), ())), preferred_element_type=F32)


def split(x):
    high = x.astype(BF16)
    return high, (x - high.astype(F32)).astype(BF16)


def level_lanes(i):
    return slice(i * RANK, (i + 1) * RANK)


def owned(i, core):
    return pl.ds(pl.multiple_of(i * PART + core * ROWS, ROWS), ROWS)


def quarter(y, k):
    return pl.ds(pl.multiple_of((y ^ k) * PART, PART), PART)


def coefficients(v, basis_ref, levels, full_ref):
    for i, level in enumerate(levels):
        full_ref[:, level_lanes(i)] = dot(v, basis_ref[level])


def own_half(core):
    return pl.ds(pl.multiple_of(core * LANES, LANES), LANES)


def scatter_halves(core, full_ref, send_ref, keep_ref, at):
    for i in range(2):
        lanes = slice(i * LANES, (i + 1) * LANES)
        half = full_ref.at[:, level_lanes(i)]
        keep_ref[:, lanes] = half[:, own_half(core)]
        send_ref[:, at + i * LANES : at + (i + 1) * LANES] = half[:, own_half(1 - core)]


def start_kernel(core_ref, v_hbm, flat_ref, basis_out, send_ref, keep_ref, low_ref, full, held, basis_ref, v_ref, sems):
    rows = LEAF * LEVELS // CHUNKS
    points = LEAF // CHUNKS
    copies = [
        pltpu.make_async_copy(
            flat_ref.at[pl.ds(i * rows, rows)], held.at[pl.ds(i * rows, rows)], sems.at[i]
        )
        for i in range(CHUNKS)
    ]
    saves = [
        pltpu.make_async_copy(
            basis_ref.at[:, pl.ds(i * points, points)],
            basis_out.at[:, pl.ds(i * points, points)],
            sems.at[CHUNKS + 1 + i],
        )
        for i in range(CHUNKS)
    ]
    last = pltpu.make_async_copy(v_hbm, v_ref, sems.at[CHUNKS])
    for copy in copies:
        copy.start()
    last.start()
    width = 32
    block = width * LEVELS
    to = lax.broadcasted_iota(jnp.int32, (block, block), 0)
    at = lax.broadcasted_iota(jnp.int32, (block, block), 1)
    source = (to & (width - 1)) * LEVELS + (to >> 5)
    order = jnp.where(at == source, 1.0, 0.0).astype(BF16)
    for i, copy in enumerate(copies):
        copy.wait()
        for j in range(i * rows // block, (i + 1) * rows // block):
            moved = dot(order, held[j * block : (j + 1) * block, :]).astype(BF16)
            for level in range(LEVELS):
                basis_ref[level, j * width : (j + 1) * width, :] = moved[
                    level * width : (level + 1) * width
                ]
        saves[i].start()
    last.wait()
    v = v_ref[...].astype(BF16)
    send_ref[:, :RANK] = dot(v, basis_ref[5])
    coefficients(v, basis_ref, (6, 7), full)
    scatter_halves(core_ref[0], full, send_ref, keep_ref, RANK)
    coefficients(v, basis_ref, (2, 3, 4), low_ref)
    for save in saves:
        save.wait()


def whole_kernel(levels, v_ref, basis_ref, gate_ref, out_ref):
    coefficients(v_ref[...].astype(BF16), basis_ref, levels, out_ref)


def parts_kernel(y_ref, low_ref, keep_ref, other_ref, *parts):
    for k, part in enumerate(parts):
        at = quarter(y_ref[0], k)
        part[:, : 3 * RANK] = low_ref[at, :]
        part[:, 3 * RANK : 4 * RANK] = other_ref[at, :RANK]
        part[:, 4 * RANK :] = keep_ref[at, :] + other_ref[at, RANK:]


def gather_kernel(order_ref, values_ref, gate_ref, out_ref):
    x = values_ref[...]
    a, rest = x.astype(BF16), x - x.astype(BF16).astype(F32)
    b, c = split(rest)
    pieces = jnp.concatenate([a, b, c], axis=0)
    step = 256
    total = None
    for i in range(LEAF // step):
        source = lax.broadcasted_iota(jnp.int32, (step, LEAF), 0) + i * step
        hot = jnp.where(source == order_ref[...], 1.0, 0.0).astype(BF16)
        term = dot(pieces[:, i * step : (i + 1) * step], hot)
        total = term if total is None else total + term
    out_ref[...] = total[:8] + total[8:16] + total[16:]


def matrix_kernel(half, values_ref, high_ref, low_ref):
    step = 128
    columns = values_ref[...].T
    for i in range(LEAF // 2 // step):
        at = slice(half * LEAF // 2 + i * step, half * LEAF // 2 + (i + 1) * step)
        square = None
        for c in range(3):
            diff = columns[at, c : c + 1] - values_ref[c : c + 1, :]
            square = diff * diff if square is None else square + diff * diff
        t = ROOT_OF_THREE * jnp.sqrt(square)
        high, low = split((1.0 + t) * jnp.exp(-t))
        high_ref[i * step : (i + 1) * step, :] = high
        low_ref[i * step : (i + 1) * step, :] = low


def near_kernel(v_ref, values_ref, high0, high1, low0, low1, *rest):
    out_ref = rest[-1]
    v = v_ref[...]
    v_high, v_low = split(v)
    both = LEAF // 2
    first, second = slice(0, both), slice(both, LEAF)
    out_ref[...] = (
        (dot(v_low[:, first], high0[...]) + dot(v_low[:, second], high1[...]))
        + (dot(v_high[:, first], low0[...]) + dot(v_high[:, second], low1[...]))
        + (dot(v_high[:, first], high0[...]) + dot(v_high[:, second], high1[...]))
        + values_ref[3:4, :] * v
    )


def base_kernel(near_ref, v_ref, basis_ref, sib0, sib1, out_ref):
    zero = (sib0[:, :RANK] * factor(0)).astype(BF16)
    one = (sib1[...] * factor(1)).astype(BF16)
    out_ref[...] = (
        (near_ref[...] - SHIFT * v_ref[...])
        + dot_t(zero, basis_ref[0])
        + dot_t(one, basis_ref[1])
    )


def far_first_kernel(y_ref, basis_ref, b0, b1, b2, b3, out_ref, held):
    for k, back in enumerate((b0, b1, b2, b3)):
        for i in range(4):
            held[quarter(y_ref[0], k), level_lanes(i)] = (
                back[:, level_lanes(i)] * factor(2 + i)
            ).astype(BF16)
    total = None
    for i in range(4):
        term = dot_t(held[:, level_lanes(i)], basis_ref[2 + i])
        total = term if total is None else total + term
    out_ref[...] = total


def far_of_halves(core, own_ref, other_ref, levels, basis_ref, held, total):
    for i in range(len(levels)):
        for ref, side in ((own_ref, core), (other_ref, 1 - core)):
            scaled = (ref[:, level_lanes(i)] * factor(levels[i])).astype(BF16)
            for j in range(4):
                held[owned(j, side), level_lanes(i)] = scaled[j * ROWS : (j + 1) * ROWS]
    for i, level in enumerate(levels):
        total += dot_t(held[:, level_lanes(i)], basis_ref[level])
    return total


def far_second_kernel(core_ref, near_ref, basis_ref, own_ref, other_ref, out_ref, held):
    out_ref[...] = far_of_halves(
        core_ref[0], own_ref, other_ref, (0, 1, 2), basis_ref, held, near_ref[...]
    )


def far_high(core, own_ref, other_ref, basis_ref, held):
    for i in range(2):
        lanes = slice(i * LANES, (i + 1) * LANES)
        half = held.at[:, level_lanes(i)]
        half[:, own_half(core)] = (own_ref[:, lanes] * factor(6 + i)).astype(BF16)
        half[:, own_half(1 - core)] = (other_ref[:, lanes] * factor(6 + i)).astype(BF16)
    return dot_t(held[:, level_lanes(0)], basis_ref[6]) + dot_t(
        held[:, level_lanes(1)], basis_ref[7]
    )


def give_halves(core, full_ref, send_ref, keep_ref):
    for i in range(4):
        to = slice(i * ROWS, (i + 1) * ROWS)
        send_ref[to, :] = full_ref[owned(i, 1 - core), :]
        keep_ref[to, :] = full_ref[owned(i, core), :]


def middle_kernel(core_ref, own_ref, other_ref, *refs):
    basis_ref, base_ref, low_ref, image_ref, far_ref, send_ref, keep_ref, held, full = refs
    core = core_ref[0]
    far = low_ref[...] + far_high(core, own_ref, other_ref, basis_ref, held)
    far_ref[...] = far
    image = base_ref[...] + far
    image_ref[...] = image
    coefficients(image.astype(BF16), basis_ref, range(LEVELS), full)
    give_halves(core, full, send_ref, keep_ref)


def dots_kernel(core_ref, base_ref, far_ref, image_ref, near_ref, v_ref, values_ref, high0, high1, gate_ref, *refs):
    send_ref, keep_ref, block_ref = refs
    far, near, image, v = far_ref[...], near_ref[...], image_ref[...], v_ref[...]
    rounded = far.astype(BF16)
    half = LEAF // 2
    own = (
        dot(rounded[:, :half], high0[...])
        + dot(rounded[:, half:], high1[...])
        + values_ref[3:4, :] * far
    )
    curve = base_ref[...] * near + far * (2.0 * near + own)
    lane = lax.broadcasted_iota(jnp.int32, (PROBES, LANES), 1)
    block = jnp.zeros((PROBES, LANES), F32)
    for i, term in enumerate((v * v, v * image, image * image, curve)):
        block = jnp.where(lane == i, jnp.sum(term, axis=1, keepdims=True), block)
    block_ref[...] = block
    give_halves(core_ref[0], block_ref, send_ref, keep_ref)


def final_kernel(core_ref, own_ref, other_ref, basis_ref, low_ref, image_ref, v_ref, x_ref, r_ref, held, dots):
    core = core_ref[0]
    for ref, side in ((own_ref, core), (other_ref, 1 - core)):
        for j in range(4):
            dots[owned(j, side), :] = ref[j * ROWS : (j + 1) * ROWS, 5 * RANK :]
    second = far_of_halves(
        core, own_ref, other_ref, (3, 4, 5, 6, 7), basis_ref, held, low_ref[...]
    )
    n0, n1, n2, n3 = (dots[:, i : i + 1] for i in range(4))
    m1 = n1 + SHIFT * n0
    mixed = n2 + SHIFT * n1
    alpha = n0 / m1
    norm = alpha * (alpha * n2 - n1 * (n1 / m1))
    curve = alpha * alpha * (n3 - mixed * (mixed / m1))
    alpha_next = norm / curve
    grown = alpha * (mixed / m1)
    v = v_ref[...]
    shifted = image_ref[...]
    image = shifted + SHIFT * v
    x_ref[...] = alpha * v + alpha_next * (grown * v - alpha * shifted)
    r_ref[...] = (n1 / m1) * v - alpha * shifted - alpha_next * (grown * image - alpha * second)


def assemble_kernel(y_ref, b0, b1, b2, b3, out_ref):
    for k, back in enumerate((b0, b1, b2, b3)):
        out_ref[quarter(y_ref[0], k), :] = back[:, 4 * RANK :]


def pair_dot(a, b, level):
    return 2.0 * factor(level) * jnp.sum(a * b, axis=1, keepdims=True)


def in_lane(i, x):
    lane = lax.broadcasted_iota(jnp.int32, (PART, LANES), 1)
    return jnp.where(lane == i, x, 0.0)


def sum_kernel(r0, r1, r2, r3, gate_ref, total_ref):
    total_ref[...] = (r0[...] + r1[...]) + (r2[...] + r3[...])


def shift_kernel(own, other, out_ref):
    out_ref[...] = own[:, RANK:] + other[:, RANK:]


def six_seven_kernel(own, other, *refs):
    six_ref, seven_ref = refs[-2:]
    six, seven = slice(2 * RANK, 2 * RANK + LANES), slice(2 * RANK + LANES, 3 * RANK)
    six_ref[...] = own[:, six] + other[:, six]
    seven_ref[...] = own[:, seven] + other[:, seven]


def join_first_kernel(two, three, four, own, x1, x2, x3, gate_ref, out_ref):
    out_ref[:, level_lanes(0)] = two[:, :RANK]
    out_ref[:, level_lanes(1)] = three[:, :RANK]
    out_ref[:, level_lanes(2)] = four[:, :RANK]
    out_ref[:, level_lanes(3)] = own[:, level_lanes(1)] + four[:, level_lanes(1)]
    out_ref[:, 4 * RANK : 4 * RANK + LANES] = x1[...]
    out_ref[:, 4 * RANK + LANES :] = x2[...] + x3[...]


def merge_kernel(y_ref, keep_ref, other_ref, keep_dots, other_dots, *parts):
    end = 6 * RANK
    for k, part_ref in enumerate(parts):
        at = pl.ds(pl.multiple_of((y_ref[0] ^ k) * ROWS, ROWS), ROWS)
        for level in range(6):
            part_ref[:, level_lanes(2 * level)] = keep_ref[at, level_lanes(level)]
            part_ref[:, level_lanes(2 * level + 1)] = other_ref[at, level_lanes(level)]
        part_ref[:, 2 * end : -LANES] = keep_ref[at, end:] + other_ref[at, end:]
        part_ref[:, -LANES:] = keep_dots[at, :] + other_dots[at, :]


def add_dot(total_ref, lane, term):
    lanes = lax.broadcasted_iota(jnp.int32, (ROWS, LANES), 1)
    total_ref[:, -LANES:] += jnp.where(lanes == lane, term, 0.0)


def y_dots_kernel(r0, r1, r2, r3, gate_ref, total_ref):
    pair = 2 * RANK
    start = 2 * pair
    total_ref[...] = (r0[:, start:] + r1[:, start:]) + (r2[:, start:] + r3[:, start:])
    a, b = slice(0, pair), slice(pair, start)
    term = pair_dot(r0[:, a], r1[:, a], 0) + pair_dot(r2[:, a], r3[:, a], 0)
    term += pair_dot(r0[:, b] + r1[:, b], r2[:, b] + r3[:, b], 1)
    add_dot(total_ref, 3, term)


def step_kernel(level, own, other, *rest):
    total_ref = rest[-1]
    pair = 2 * RANK
    total_ref[...] = own[:, pair:] + other[:, pair:]
    add_dot(total_ref, 3, pair_dot(own[:, :pair], other[:, :pair], level))


def last_step_kernel(own, other, g1, g2, g3, five_ref, total_ref):
    pair = 2 * RANK
    term = pair_dot(own[:, :pair], other[:, :pair], 4)
    five_ref[...] = own[:, pair : 2 * pair] + other[:, pair : 2 * pair]
    total_ref[...] = own[:, 2 * pair :] + other[:, 2 * pair :]
    term += pair_dot(five_ref[:, level_lanes(0)], five_ref[:, level_lanes(1)], 5)
    add_dot(total_ref, 3, term)


def low_join_kernel(r0, r1, r2, r3, two, gate_ref, *outs):
    r = (r0, r1, r2, r3)
    pair = 2 * RANK
    zero, one = slice(0, pair), slice(pair, 2 * pair)
    for k, out in enumerate(outs):
        out[:, zero] = r[k ^ 1][:, zero]
        out[:, one] = r[k ^ 2][:, one] + r[k ^ 3][:, one]
        out[:, 2 * pair :] = two[:, :pair]


def high_join_kernel(three, four, five, own, x1, x2, x3, out_ref):
    a, b, q = slice(0, RANK), slice(RANK, 2 * RANK), slice(2 * RANK, 2 * RANK + LANES)
    far = x2[:, b] + x3[:, b]
    pair = 2 * RANK
    out_ref[:, :pair] = three[:, :pair]
    out_ref[:, pair : 2 * pair] = four[:, :pair]
    out_ref[:, level_lanes(4)] = five[:, level_lanes(1)]
    out_ref[:, level_lanes(5)] = five[:, level_lanes(0)]
    out_ref[:, level_lanes(6)] = x1[:, a]
    out_ref[:, level_lanes(7)] = far
    out_ref[:, 8 * RANK :] = (own[:, q] + x1[:, q]) + (x2[:, q] + x3[:, q])
    term = pair_dot(own[:, a], x1[:, a], 6) + pair_dot(x2[:, a], x3[:, a], 6)
    term += pair_dot(own[:, b] + x1[:, b], far, 7)
    add_dot(out_ref, 3, term)


def gather_kernel_of(levels, shared, y_ref, b0, b1, b2, b3, *rest):
    own_ref, send_ref = rest[-2:]
    for k, back in enumerate((b0, b1, b2, b3)):
        at = pl.ds(pl.multiple_of((y_ref[0] ^ k) * ROWS, ROWS), ROWS)
        for i in range(levels):
            own_ref[at, level_lanes(i)] = back[:, level_lanes(2 * i)]
            send_ref[at, level_lanes(i)] = back[:, level_lanes(2 * i + 1)]
        if shared:
            own_ref[at, levels * RANK :] = back[:, 2 * levels * RANK :]
            send_ref[at, levels * RANK :] = back[:, 2 * levels * RANK :]


def swap(x, axis, mask):
    return lax.ppermute(x, axis, [(i, i ^ mask) for i in range(lax.axis_size(axis))])


def over_y(x):
    return [x[0]] + [swap(x[k], "local", k) for k in (1, 2, 3)]


Z1, Z2, Z3 = ("local", 4), ("local", 8), ("local", 24)
CORE, X1, X2, X3 = ("group", 1), ("group", 2), ("group", 4), ("group", 6)


def rows(lanes):
    return shape(ROWS, lanes)


def part(lanes):
    return shape(PART, lanes)


def per_device(coords, inv_length, noise, order, basis, probes):
    y = (lax.axis_index("local") & 3).astype(jnp.int32)[None]
    core = (lax.axis_index("group") & 1).astype(jnp.int32)[None]
    flat = basis.reshape(LEAF * LEVELS, RANK)
    square = shape(LEAF // 2, LEAF, dtype=BF16)
    vectors = shape(PROBES, LEAF)
    both = shape(PROBES, RANK)

    basis, send, keep, low = call(
        start_kernel,
        (
            shape(LEVELS, LEAF, RANK, dtype=BF16),
            shape(PROBES, 2 * RANK),
            both,
            shape(PROBES, 3 * RANK),
        ),
        core,
        pltpu.with_memory_space_constraint(probes, pltpu.HBM),
        pltpu.with_memory_space_constraint(flat, pltpu.HBM),
        scratch=[
            pltpu.VMEM((PROBES, 2 * RANK), F32),
            pltpu.VMEM((LEAF * LEVELS, RANK), BF16),
            pltpu.VMEM((LEVELS, LEAF, RANK), BF16),
            pltpu.VMEM((PROBES, LEAF), F32),
            pltpu.SemaphoreType.DMA((2 * CHUNKS + 1,)),
        ],
        smem=1,
        outside=2,
        flops=2**31,
        limit=START_LIMIT,
        outs=(ANY, VMEM, VMEM, VMEM),
    )
    other = swap(send, *CORE)
    parts = call(parts_kernel, (part(5 * RANK),) * 4, y, low, keep, other, smem=1)
    moved = over_y(parts)

    values = jnp.concatenate(
        [coords * inv_length[:, None], noise[None, :], jnp.zeros((4, LEAF), F32)], axis=0
    )
    values = call(
        gather_kernel, shape(8, LEAF), order, values, parts[0], anywhere=1, flops=2**26
    )
    high0, low0 = call(
        functools.partial(matrix_kernel, 0), (square, square), values, flops=2**30
    )
    high1, low1 = call(
        functools.partial(matrix_kernel, 1), (square, square), values, flops=2**30
    )
    matrix = (values, high0, high1, low0, low1)
    near = call(near_kernel, vectors, probes, *matrix, flops=2**30)

    total = call(sum_kernel, part(5 * RANK), *moved, near, anywhere=1)
    two = swap(total, *Z1)
    leaf = call(
        functools.partial(whole_kernel, (0, 1)),
        shape(PROBES, 2 * RANK),
        probes,
        basis,
        total,
        anywhere=1,
        flops=2**28,
    )
    leaf_other = swap(leaf, "local", 1)
    total = call(shift_kernel, part(4 * RANK), total, two)
    three = swap(total, *Z2)
    leaf_next = call(shift_kernel, both, leaf, leaf_other)
    one = swap(leaf_next, "local", 3)
    total = call(shift_kernel, part(3 * RANK), total, three)
    four = swap(total, *Z3)
    six, seven = call(
        six_seven_kernel, (part(LANES),) * 2, total, four, one, anywhere=1
    )
    x1, x2, x3 = swap(six, *X1), swap(seven, *X2), swap(seven, *X3)
    base = call(
        base_kernel, vectors, near, probes, basis, leaf_other, one, flops=2**28
    )
    base_near = call(near_kernel, vectors, base, *matrix, flops=2**30)
    back = call(
        join_first_kernel,
        part(5 * RANK),
        two,
        three,
        four,
        total,
        x1,
        x2,
        x3,
        base_near,
        anywhere=1,
    )
    back = over_y([back] * 4)
    own = call(assemble_kernel, both, y, *back, smem=1)
    other = swap(own, *CORE)
    far = call(
        far_first_kernel,
        vectors,
        y,
        basis,
        *back,
        scratch=[pltpu.VMEM((PROBES, 4 * RANK), BF16)],
        smem=1,
        flops=2**29,
    )
    wide, half = LEVELS * RANK, PROBES // 2
    image, far, send, keep = call(
        middle_kernel,
        (vectors, vectors, shape(half, wide), shape(half, wide)),
        core,
        own,
        other,
        basis,
        base,
        far,
        scratch=[pltpu.VMEM((PROBES, 2 * RANK), BF16), pltpu.VMEM((PROBES, wide), F32)],
        smem=1,
        flops=2**30,
    )
    other = swap(send, *CORE)
    send, keep_dots = call(
        dots_kernel,
        (shape(half, LANES), shape(half, LANES)),
        core,
        base,
        far,
        image,
        base_near,
        probes,
        values,
        high0,
        high1,
        send,
        scratch=[pltpu.VMEM((PROBES, LANES), F32)],
        smem=1,
        anywhere=1,
        flops=2**28,
    )
    other_dots = swap(send, *CORE)
    parts = call(
        merge_kernel,
        (rows(14 * RANK + LANES),) * 4,
        y,
        keep,
        other,
        keep_dots,
        other_dots,
        smem=1,
    )
    moved = over_y(parts)
    near = call(
        near_kernel, vectors, image, *matrix, parts[0], anywhere=1, flops=2**30
    )
    total = call(
        y_dots_kernel, rows(10 * RANK + LANES), *moved, near, anywhere=1
    )
    two = swap(total, *Z1)
    total = call(functools.partial(step_kernel, 2), rows(8 * RANK + LANES), total, two)
    three = swap(total, *Z2)
    back = call(low_join_kernel, (rows(6 * RANK),) * 4, *moved, two, total, anywhere=1)
    back = over_y(back)
    total = call(functools.partial(step_kernel, 3), rows(6 * RANK + LANES), total, three)
    four = swap(total, *Z3)
    five, total = call(
        last_step_kernel,
        (rows(2 * RANK), rows(2 * RANK + LANES)),
        total,
        four,
        *back[1:],
        anywhere=3,
    )
    x1, x2, x3 = swap(total, *X1), swap(total, *X2), swap(total, *X3)
    low_own, send = call(
        functools.partial(gather_kernel_of, 3, False),
        (shape(PROBES // 2, 3 * RANK),) * 2,
        y,
        *back,
        smem=1,
    )
    low_other = swap(send, *CORE)
    high_back = call(
        high_join_kernel, rows(8 * RANK + LANES), three, four, five, total, x1, x2, x3
    )
    high_back = over_y([high_back] * 4)
    partial_second = call(
        far_second_kernel,
        vectors,
        core,
        near,
        basis,
        low_own,
        low_other,
        scratch=[pltpu.VMEM((PROBES, 3 * RANK), BF16)],
        smem=1,
        flops=2**29,
    )
    own, send = call(
        functools.partial(gather_kernel_of, 3, True),
        (shape(PROBES // 2, 5 * RANK + LANES),) * 2,
        y,
        *high_back,
        partial_second,
        smem=1,
        anywhere=1,
    )
    other = swap(send, *CORE)
    return call(
        final_kernel,
        (vectors, vectors),
        core,
        own,
        other,
        basis,
        partial_second,
        image,
        probes,
        scratch=[pltpu.VMEM((PROBES, 5 * RANK), BF16), pltpu.VMEM((PROBES, LANES), F32)],
        smem=1,
        flops=2**29,
    )


def solution(mesh):
    in_specs = (
        P(None, ("group", "local")),
        P(),
        P(("group", "local")),
        P(("group", "local"), None),
        P(("group", "local"), None, None),
        P(None, ("group", "local")),
    )
    out_specs = (P(None, ("group", "local")), P(None, ("group", "local")))
    return jax.shard_map(
        per_device, mesh=mesh, in_specs=in_specs, out_specs=out_specs, check_vma=False
    )
```

```python
import functools
import math

import jax
import jax.numpy as jnp
from jax import lax
from jax.experimental import pallas as pl
from jax.experimental.pallas import tpu as pltpu
from jax.sharding import PartitionSpec as P

GAMMA = 0.08
ROOT_OF_THREE = math.sqrt(3.0)
SHIFT = 3.5
LEVELS = 8
RANK = 256
LEAF = 1024
PROBES = 128
PART = PROBES // 4
ROWS = PART // 2
LANES = 128
CHUNKS = 2
START_LIMIT = 52
F32 = jnp.float32
BF16 = jnp.bfloat16
VMEM = pl.BlockSpec(memory_space=pltpu.VMEM)
SMEM = pl.BlockSpec(memory_space=pltpu.SMEM)
ANY = pl.BlockSpec(memory_space=pl.ANY)
HBM = pl.BlockSpec(memory_space=pltpu.HBM)


def factor(level):
    return GAMMA / (LEAF * 2.0**level)


def call(kernel, out_shape, *args, scratch=(), smem=0, anywhere=0, outside=0, flops=0, limit=16, outs=None):
    held = len(args) - smem - anywhere - outside
    return pl.pallas_call(
        kernel,
        out_shape=out_shape,
        in_specs=[SMEM] * smem + [VMEM] * held + [ANY] * anywhere + [HBM] * outside,
        out_specs=outs or jax.tree.map(lambda _: VMEM, out_shape),
        scratch_shapes=list(scratch),
        compiler_params=pltpu.CompilerParams(vmem_limit_bytes=limit * 2**20),
        cost_estimate=pl.CostEstimate(
            flops=flops, bytes_accessed=2**20, transcendentals=0
        ),
    )(*args)


def shape(*dims, dtype=F32):
    return jax.ShapeDtypeStruct(dims, dtype)


def dot(a, b):
    return jnp.dot(a, b, preferred_element_type=F32)


def dot_t(a, b):
    return lax.dot_general(a, b, (((1,), (1,)), ((), ())), preferred_element_type=F32)


def split(x):
    high = x.astype(BF16)
    return high, (x - high.astype(F32)).astype(BF16)


def level_lanes(i):
    return slice(i * RANK, (i + 1) * RANK)


def owned(i, core):
    return pl.ds(pl.multiple_of(i * PART + core * ROWS, ROWS), ROWS)


def quarter(y, k):
    return pl.ds(pl.multiple_of((y ^ k) * PART, PART), PART)


def coefficients(v, basis_ref, levels, full_ref):
    for i, level in enumerate(levels):
        full_ref[:, level_lanes(i)] = dot(v, basis_ref[level])


def own_half(core):
    return pl.ds(pl.multiple_of(core * LANES, LANES), LANES)


def scatter_halves(core, full_ref, send_ref, keep_ref, at):
    for i in range(2):
        lanes = slice(i * LANES, (i + 1) * LANES)
        half = full_ref.at[:, level_lanes(i)]
        keep_ref[:, lanes] = half[:, own_half(core)]
        send_ref[:, at + i * LANES : at + (i + 1) * LANES] = half[:, own_half(1 - core)]


def start_kernel(core_ref, v_hbm, flat_ref, basis_out, send_ref, keep_ref, low_ref, full, held, basis_ref, v_ref, sems):
    rows = LEAF * LEVELS // CHUNKS
    points = LEAF // CHUNKS
    copies = [
        pltpu.make_async_copy(
            flat_ref.at[pl.ds(i * rows, rows)], held.at[pl.ds(i * rows, rows)], sems.at[i]
        )
        for i in range(CHUNKS)
    ]
    saves = [
        pltpu.make_async_copy(
            basis_ref.at[:, pl.ds(i * points, points)],
            basis_out.at[:, pl.ds(i * points, points)],
            sems.at[CHUNKS + 1 + i],
        )
        for i in range(CHUNKS)
    ]
    last = pltpu.make_async_copy(v_hbm, v_ref, sems.at[CHUNKS])
    for copy in copies:
        copy.start()
    last.start()
    width = 32
    block = width * LEVELS
    to = lax.broadcasted_iota(jnp.int32, (block, block), 0)
    at = lax.broadcasted_iota(jnp.int32, (block, block), 1)
    source = (to & (width - 1)) * LEVELS + (to >> 5)
    order = jnp.where(at == source, 1.0, 0.0).astype(BF16)
    for i, copy in enumerate(copies):
        copy.wait()
        for j in range(i * rows // block, (i + 1) * rows // block):
            moved = dot(order, held[j * block : (j + 1) * block, :]).astype(BF16)
            for level in range(LEVELS):
                basis_ref[level, j * width : (j + 1) * width, :] = moved[
                    level * width : (level + 1) * width
                ]
        saves[i].start()
    last.wait()
    v = v_ref[...].astype(BF16)
    send_ref[:, :RANK] = dot(v, basis_ref[5])
    coefficients(v, basis_ref, (6, 7), full)
    scatter_halves(core_ref[0], full, send_ref, keep_ref, RANK)
    coefficients(v, basis_ref, (2, 3, 4), low_ref)
    for save in saves:
        save.wait()


def whole_kernel(levels, v_ref, basis_ref, gate_ref, out_ref):
    coefficients(v_ref[...].astype(BF16), basis_ref, levels, out_ref)


def parts_kernel(y_ref, low_ref, keep_ref, other_ref, *parts):
    for k, part in enumerate(parts):
        at = quarter(y_ref[0], k)
        part[:, : 3 * RANK] = low_ref[at, :]
        part[:, 3 * RANK : 4 * RANK] = other_ref[at, :RANK]
        part[:, 4 * RANK :] = keep_ref[at, :] + other_ref[at, RANK:]


def gather_kernel(order_ref, values_ref, gate_ref, out_ref):
    x = values_ref[...]
    a, rest = x.astype(BF16), x - x.astype(BF16).astype(F32)
    b, c = split(rest)
    pieces = jnp.concatenate([a, b, c], axis=0)
    step = 256
    total = None
    for i in range(LEAF // step):
        source = lax.broadcasted_iota(jnp.int32, (step, LEAF), 0) + i * step
        hot = jnp.where(source == order_ref[...], 1.0, 0.0).astype(BF16)
        term = dot(pieces[:, i * step : (i + 1) * step], hot)
        total = term if total is None else total + term
    out_ref[...] = total[:8] + total[8:16] + total[16:]


def matrix_kernel(half, values_ref, high_ref, low_ref):
    step = 128
    columns = values_ref[...].T
    for i in range(LEAF // 2 // step):
        at = slice(half * LEAF // 2 + i * step, half * LEAF // 2 + (i + 1) * step)
        square = None
        for c in range(3):
            diff = columns[at, c : c + 1] - values_ref[c : c + 1, :]
            square = diff * diff if square is None else square + diff * diff
        t = ROOT_OF_THREE * jnp.sqrt(square)
        high, low = split((1.0 + t) * jnp.exp(-t))
        high_ref[i * step : (i + 1) * step, :] = high
        low_ref[i * step : (i + 1) * step, :] = low


def near_kernel(v_ref, values_ref, high0, high1, low0, low1, *rest):
    out_ref = rest[-1]
    v = v_ref[...]
    v_high, v_low = split(v)
    both = LEAF // 2
    first, second = slice(0, both), slice(both, LEAF)
    out_ref[...] = (
        (dot(v_low[:, first], high0[...]) + dot(v_low[:, second], high1[...]))
        + (dot(v_high[:, first], low0[...]) + dot(v_high[:, second], low1[...]))
        + (dot(v_high[:, first], high0[...]) + dot(v_high[:, second], high1[...]))
        + values_ref[3:4, :] * v
    )


def base_kernel(near_ref, v_ref, basis_ref, sib0, sib1, out_ref):
    zero = (sib0[:, :RANK] * factor(0)).astype(BF16)
    one = (sib1[...] * factor(1)).astype(BF16)
    out_ref[...] = (
        (near_ref[...] - SHIFT * v_ref[...])
        + dot_t(zero, basis_ref[0])
        + dot_t(one, basis_ref[1])
    )


def far_first_kernel(y_ref, basis_ref, b0, b1, b2, b3, out_ref, held):
    for k, back in enumerate((b0, b1, b2, b3)):
        for i in range(4):
            held[quarter(y_ref[0], k), level_lanes(i)] = (
                back[:, level_lanes(i)] * factor(2 + i)
            ).astype(BF16)
    total = None
    for i in range(4):
        term = dot_t(held[:, level_lanes(i)], basis_ref[2 + i])
        total = term if total is None else total + term
    out_ref[...] = total


def far_of_halves(core, own_ref, other_ref, levels, basis_ref, held, total):
    for i in range(len(levels)):
        for ref, side in ((own_ref, core), (other_ref, 1 - core)):
            scaled = (ref[:, level_lanes(i)] * factor(levels[i])).astype(BF16)
            for j in range(4):
                held[owned(j, side), level_lanes(i)] = scaled[j * ROWS : (j + 1) * ROWS]
    for i, level in enumerate(levels):
        total += dot_t(held[:, level_lanes(i)], basis_ref[level])
    return total


def far_second_kernel(core_ref, near_ref, basis_ref, own_ref, other_ref, out_ref, held):
    out_ref[...] = far_of_halves(
        core_ref[0], own_ref, other_ref, (0, 1, 2), basis_ref, held, near_ref[...]
    )


def far_high(core, own_ref, other_ref, basis_ref, held):
    for i in range(2):
        lanes = slice(i * LANES, (i + 1) * LANES)
        half = held.at[:, level_lanes(i)]
        half[:, own_half(core)] = (own_ref[:, lanes] * factor(6 + i)).astype(BF16)
        half[:, own_half(1 - core)] = (other_ref[:, lanes] * factor(6 + i)).astype(BF16)
    return dot_t(held[:, level_lanes(0)], basis_ref[6]) + dot_t(
        held[:, level_lanes(1)], basis_ref[7]
    )


def give_halves(core, full_ref, send_ref, keep_ref):
    for i in range(4):
        to = slice(i * ROWS, (i + 1) * ROWS)
        send_ref[to, :] = full_ref[owned(i, 1 - core), :]
        keep_ref[to, :] = full_ref[owned(i, core), :]


def middle_kernel(core_ref, own_ref, other_ref, *refs):
    basis_ref, base_ref, low_ref, image_ref, far_ref, send_ref, keep_ref, held, full = refs
    core = core_ref[0]
    far = low_ref[...] + far_high(core, own_ref, other_ref, basis_ref, held)
    far_ref[...] = far
    image = base_ref[...] + far
    image_ref[...] = image
    coefficients(image.astype(BF16), basis_ref, range(LEVELS), full)
    give_halves(core, full, send_ref, keep_ref)


def dots_kernel(core_ref, base_ref, far_ref, image_ref, near_ref, v_ref, values_ref, high0, high1, gate_ref, *refs):
    send_ref, keep_ref, block_ref = refs
    far, near, image, v = far_ref[...], near_ref[...], image_ref[...], v_ref[...]
    rounded = far.astype(BF16)
    half = LEAF // 2
    own = (
        dot(rounded[:, :half], high0[...])
        + dot(rounded[:, half:], high1[...])
        + values_ref[3:4, :] * far
    )
    curve = base_ref[...] * near + far * (2.0 * near + own)
    lane = lax.broadcasted_iota(jnp.int32, (PROBES, LANES), 1)
    block = jnp.zeros((PROBES, LANES), F32)
    for i, term in enumerate((v * v, v * image, image * image, curve)):
        block = jnp.where(lane == i, jnp.sum(term, axis=1, keepdims=True), block)
    block_ref[...] = block
    give_halves(core_ref[0], block_ref, send_ref, keep_ref)


def final_kernel(core_ref, own_ref, other_ref, basis_ref, low_ref, image_ref, v_ref, x_ref, r_ref, held, dots):
    core = core_ref[0]
    for ref, side in ((own_ref, core), (other_ref, 1 - core)):
        for j in range(4):
            dots[owned(j, side), :] = ref[j * ROWS : (j + 1) * ROWS, 5 * RANK :]
    second = far_of_halves(
        core, own_ref, other_ref, (3, 4, 5, 6, 7), basis_ref, held, low_ref[...]
    )
    n0, n1, n2, n3 = (dots[:, i : i + 1] for i in range(4))
    m1 = n1 + SHIFT * n0
    mixed = n2 + SHIFT * n1
    alpha = n0 / m1
    norm = alpha * (alpha * n2 - n1 * (n1 / m1))
    curve = alpha * alpha * (n3 - mixed * (mixed / m1))
    alpha_next = norm / curve
    grown = alpha * (mixed / m1)
    v = v_ref[...]
    shifted = image_ref[...]
    image = shifted + SHIFT * v
    x_ref[...] = alpha * v + alpha_next * (grown * v - alpha * shifted)
    r_ref[...] = (n1 / m1) * v - alpha * shifted - alpha_next * (grown * image - alpha * second)


def assemble_kernel(y_ref, b0, b1, b2, b3, out_ref):
    for k, back in enumerate((b0, b1, b2, b3)):
        out_ref[quarter(y_ref[0], k), :] = back[:, 4 * RANK :]


def pair_dot(a, b, level):
    return 2.0 * factor(level) * jnp.sum(a * b, axis=1, keepdims=True)


def in_lane(i, x):
    lane = lax.broadcasted_iota(jnp.int32, (PART, LANES), 1)
    return jnp.where(lane == i, x, 0.0)


def sum_kernel(r0, r1, r2, r3, gate_ref, total_ref):
    total_ref[...] = (r0[...] + r1[...]) + (r2[...] + r3[...])


def shift_kernel(own, other, out_ref):
    out_ref[...] = own[:, RANK:] + other[:, RANK:]


def six_seven_kernel(own, other, *refs):
    six_ref, seven_ref = refs[-2:]
    six, seven = slice(2 * RANK, 2 * RANK + LANES), slice(2 * RANK + LANES, 3 * RANK)
    six_ref[...] = own[:, six] + other[:, six]
    seven_ref[...] = own[:, seven] + other[:, seven]


def join_first_kernel(two, three, four, own, x1, x2, x3, gate_ref, out_ref):
    out_ref[:, level_lanes(0)] = two[:, :RANK]
    out_ref[:, level_lanes(1)] = three[:, :RANK]
    out_ref[:, level_lanes(2)] = four[:, :RANK]
    out_ref[:, level_lanes(3)] = own[:, level_lanes(1)] + four[:, level_lanes(1)]
    out_ref[:, 4 * RANK : 4 * RANK + LANES] = x1[...]
    out_ref[:, 4 * RANK + LANES :] = x2[...] + x3[...]


def merge_kernel(y_ref, keep_ref, other_ref, keep_dots, other_dots, *parts):
    end = 6 * RANK
    for k, part_ref in enumerate(parts):
        at = pl.ds(pl.multiple_of((y_ref[0] ^ k) * ROWS, ROWS), ROWS)
        for level in range(6):
            part_ref[:, level_lanes(2 * level)] = keep_ref[at, level_lanes(level)]
            part_ref[:, level_lanes(2 * level + 1)] = other_ref[at, level_lanes(level)]
        part_ref[:, 2 * end : -LANES] = keep_ref[at, end:] + other_ref[at, end:]
        part_ref[:, -LANES:] = keep_dots[at, :] + other_dots[at, :]


def add_dot(total_ref, lane, term):
    lanes = lax.broadcasted_iota(jnp.int32, (ROWS, LANES), 1)
    total_ref[:, -LANES:] += jnp.where(lanes == lane, term, 0.0)


def y_dots_kernel(r0, r1, r2, r3, gate_ref, total_ref):
    pair = 2 * RANK
    start = 2 * pair
    total_ref[...] = (r0[:, start:] + r1[:, start:]) + (r2[:, start:] + r3[:, start:])
    a, b = slice(0, pair), slice(pair, start)
    term = pair_dot(r0[:, a], r1[:, a], 0) + pair_dot(r2[:, a], r3[:, a], 0)
    term += pair_dot(r0[:, b] + r1[:, b], r2[:, b] + r3[:, b], 1)
    add_dot(total_ref, 3, term)


def step_kernel(level, own, other, *rest):
    total_ref = rest[-1]
    pair = 2 * RANK
    total_ref[...] = own[:, pair:] + other[:, pair:]
    add_dot(total_ref, 3, pair_dot(own[:, :pair], other[:, :pair], level))


def last_step_kernel(own, other, g1, g2, g3, five_ref, total_ref):
    pair = 2 * RANK
    term = pair_dot(own[:, :pair], other[:, :pair], 4)
    five_ref[...] = own[:, pair : 2 * pair] + other[:, pair : 2 * pair]
    total_ref[...] = own[:, 2 * pair :] + other[:, 2 * pair :]
    term += pair_dot(five_ref[:, level_lanes(0)], five_ref[:, level_lanes(1)], 5)
    add_dot(total_ref, 3, term)


def low_join_kernel(r0, r1, r2, r3, two, gate_ref, *outs):
    r = (r0, r1, r2, r3)
    pair = 2 * RANK
    zero, one = slice(0, pair), slice(pair, 2 * pair)
    for k, out in enumerate(outs):
        out[:, zero] = r[k ^ 1][:, zero]
        out[:, one] = r[k ^ 2][:, one] + r[k ^ 3][:, one]
        out[:, 2 * pair :] = two[:, :pair]


def high_join_kernel(three, four, five, own, x1, x2, x3, out_ref):
    a, b, q = slice(0, RANK), slice(RANK, 2 * RANK), slice(2 * RANK, 2 * RANK + LANES)
    far = x2[:, b] + x3[:, b]
    pair = 2 * RANK
    out_ref[:, :pair] = three[:, :pair]
    out_ref[:, pair : 2 * pair] = four[:, :pair]
    out_ref[:, level_lanes(4)] = five[:, level_lanes(1)]
    out_ref[:, level_lanes(5)] = five[:, level_lanes(0)]
    out_ref[:, level_lanes(6)] = x1[:, a]
    out_ref[:, level_lanes(7)] = far
    out_ref[:, 8 * RANK :] = (own[:, q] + x1[:, q]) + (x2[:, q] + x3[:, q])
    term = pair_dot(own[:, a], x1[:, a], 6) + pair_dot(x2[:, a], x3[:, a], 6)
    term += pair_dot(own[:, b] + x1[:, b], far, 7)
    add_dot(out_ref, 3, term)


def gather_kernel_of(levels, shared, y_ref, b0, b1, b2, b3, *rest):
    own_ref, send_ref = rest[-2:]
    for k, back in enumerate((b0, b1, b2, b3)):
        at = pl.ds(pl.multiple_of((y_ref[0] ^ k) * ROWS, ROWS), ROWS)
        for i in range(levels):
            own_ref[at, level_lanes(i)] = back[:, level_lanes(2 * i)]
            send_ref[at, level_lanes(i)] = back[:, level_lanes(2 * i + 1)]
        if shared:
            own_ref[at, levels * RANK :] = back[:, 2 * levels * RANK :]
            send_ref[at, levels * RANK :] = back[:, 2 * levels * RANK :]


def swap(x, axis, mask):
    return lax.ppermute(x, axis, [(i, i ^ mask) for i in range(lax.axis_size(axis))])


def over_y(x):
    return [x[0]] + [swap(x[k], "local", k) for k in (1, 2, 3)]


Z1, Z2, Z3 = ("local", 4), ("local", 8), ("local", 24)
CORE, X1, X2, X3 = ("group", 1), ("group", 2), ("group", 4), ("group", 6)


def rows(lanes):
    return shape(ROWS, lanes)


def part(lanes):
    return shape(PART, lanes)


def per_device(coords, inv_length, noise, order, basis, probes):
    y = (lax.axis_index("local") & 3).astype(jnp.int32)[None]
    core = (lax.axis_index("group") & 1).astype(jnp.int32)[None]
    flat = basis.reshape(LEAF * LEVELS, RANK)
    square = shape(LEAF // 2, LEAF, dtype=BF16)
    vectors = shape(PROBES, LEAF)
    both = shape(PROBES, RANK)

    basis, send, keep, low = call(
        start_kernel,
        (
            shape(LEVELS, LEAF, RANK, dtype=BF16),
            shape(PROBES, 2 * RANK),
            both,
            shape(PROBES, 3 * RANK),
        ),
        core,
        pltpu.with_memory_space_constraint(probes, pltpu.HBM),
        pltpu.with_memory_space_constraint(flat, pltpu.HBM),
        scratch=[
            pltpu.VMEM((PROBES, 2 * RANK), F32),
            pltpu.VMEM((LEAF * LEVELS, RANK), BF16),
            pltpu.VMEM((LEVELS, LEAF, RANK), BF16),
            pltpu.VMEM((PROBES, LEAF), F32),
            pltpu.SemaphoreType.DMA((2 * CHUNKS + 1,)),
        ],
        smem=1,
        outside=2,
        flops=2**31,
        limit=START_LIMIT,
        outs=(ANY, VMEM, VMEM, VMEM),
    )
    other = swap(send, *CORE)
    parts = call(parts_kernel, (part(5 * RANK),) * 4, y, low, keep, other, smem=1)
    moved = over_y(parts)

    values = jnp.concatenate(
        [coords * inv_length[:, None], noise[None, :], jnp.zeros((4, LEAF), F32)], axis=0
    )
    values = call(
        gather_kernel, shape(8, LEAF), order, values, parts[0], anywhere=1, flops=2**26
    )
    high0, low0 = call(
        functools.partial(matrix_kernel, 0), (square, square), values, flops=2**30
    )
    high1, low1 = call(
        functools.partial(matrix_kernel, 1), (square, square), values, flops=2**30
    )
    matrix = (values, high0, high1, low0, low1)
    near = call(near_kernel, vectors, probes, *matrix, flops=2**30)

    total = call(sum_kernel, part(5 * RANK), *moved, near, anywhere=1)
    two = swap(total, *Z1)
    leaf = call(
        functools.partial(whole_kernel, (0, 1)),
        shape(PROBES, 2 * RANK),
        probes,
        basis,
        total,
        anywhere=1,
        flops=2**28,
    )
    leaf_other = swap(leaf, "local", 1)
    total = call(shift_kernel, part(4 * RANK), total, two)
    three = swap(total, *Z2)
    leaf_next = call(shift_kernel, both, leaf, leaf_other)
    one = swap(leaf_next, "local", 3)
    total = call(shift_kernel, part(3 * RANK), total, three)
    four = swap(total, *Z3)
    six, seven = call(
        six_seven_kernel, (part(LANES),) * 2, total, four, one, anywhere=1
    )
    x1, x2, x3 = swap(six, *X1), swap(seven, *X2), swap(seven, *X3)
    base = call(
        base_kernel, vectors, near, probes, basis, leaf_other, one, flops=2**28
    )
    base_near = call(near_kernel, vectors, base, *matrix, flops=2**30)
    back = call(
        join_first_kernel,
        part(5 * RANK),
        two,
        three,
        four,
        total,
        x1,
        x2,
        x3,
        base_near,
        anywhere=1,
    )
    back = over_y([back] * 4)
    own = call(assemble_kernel, both, y, *back, smem=1)
    other = swap(own, *CORE)
    far = call(
        far_first_kernel,
        vectors,
        y,
        basis,
        *back,
        scratch=[pltpu.VMEM((PROBES, 4 * RANK), BF16)],
        smem=1,
        flops=2**29,
    )
    wide, half = LEVELS * RANK, PROBES // 2
    image, far, send, keep = call(
        middle_kernel,
        (vectors, vectors, shape(half, wide), shape(half, wide)),
        core,
        own,
        other,
        basis,
        base,
        far,
        scratch=[pltpu.VMEM((PROBES, 2 * RANK), BF16), pltpu.VMEM((PROBES, wide), F32)],
        smem=1,
        flops=2**30,
    )
    other = swap(send, *CORE)
    send, keep_dots = call(
        dots_kernel,
        (shape(half, LANES), shape(half, LANES)),
        core,
        base,
        far,
        image,
        base_near,
        probes,
        values,
        high0,
        high1,
        send,
        scratch=[pltpu.VMEM((PROBES, LANES), F32)],
        smem=1,
        anywhere=1,
        flops=2**28,
    )
    other_dots = swap(send, *CORE)
    parts = call(
        merge_kernel,
        (rows(14 * RANK + LANES),) * 4,
        y,
        keep,
        other,
        keep_dots,
        other_dots,
        smem=1,
    )
    moved = over_y(parts)
    near = call(
        near_kernel, vectors, image, *matrix, parts[0], anywhere=1, flops=2**30
    )
    total = call(
        y_dots_kernel, rows(10 * RANK + LANES), *moved, near, anywhere=1
    )
    two = swap(total, *Z1)
    total = call(functools.partial(step_kernel, 2), rows(8 * RANK + LANES), total, two)
    three = swap(total, *Z2)
    back = call(low_join_kernel, (rows(6 * RANK),) * 4, *moved, two, total, anywhere=1)
    back = over_y(back)
    total = call(functools.partial(step_kernel, 3), rows(6 * RANK + LANES), total, three)
    four = swap(total, *Z3)
    five, total = call(
        last_step_kernel,
        (rows(2 * RANK), rows(2 * RANK + LANES)),
        total,
        four,
        *back[1:],
        anywhere=3,
    )
    x1, x2, x3 = swap(total, *X1), swap(total, *X2), swap(total, *X3)
    low_own, send = call(
        functools.partial(gather_kernel_of, 3, False),
        (shape(PROBES // 2, 3 * RANK),) * 2,
        y,
        *back,
        smem=1,
    )
    low_other = swap(send, *CORE)
    high_back = call(
        high_join_kernel, rows(8 * RANK + LANES), three, four, five, total, x1, x2, x3
    )
    high_back = over_y([high_back] * 4)
    partial_second = call(
        far_second_kernel,
        vectors,
        core,
        near,
        basis,
        low_own,
        low_other,
        scratch=[pltpu.VMEM((PROBES, 3 * RANK), BF16)],
        smem=1,
        flops=2**29,
    )
    own, send = call(
        functools.partial(gather_kernel_of, 3, True),
        (shape(PROBES // 2, 5 * RANK + LANES),) * 2,
        y,
        *high_back,
        partial_second,
        smem=1,
        anywhere=1,
    )
    other = swap(send, *CORE)
    return call(
        final_kernel,
        (vectors, vectors),
        core,
        own,
        other,
        basis,
        partial_second,
        image,
        probes,
        scratch=[pltpu.VMEM((PROBES, 5 * RANK), BF16), pltpu.VMEM((PROBES, LANES), F32)],
        smem=1,
        flops=2**29,
    )


def solution(mesh):
    in_specs = (
        P(None, ("group", "local")),
        P(),
        P(("group", "local")),
        P(("group", "local"), None),
        P(("group", "local"), None, None),
        P(None, ("group", "local")),
    )
    out_specs = (P(None, ("group", "local")), P(None, ("group", "local")))
    return jax.shard_map(
        per_device, mesh=mesh, in_specs=in_specs, out_specs=out_specs, check_vma=False
    )
```
